512 devices in a mesh: dp: 32 (over z_hi, y, x), seq: 16 (over z_lo, core).
Axes of the slice: x: 4, y: 4, z: 16 (z_hi: 2, z_lo: 8; z = z_hi * 8 + z_lo), core: 2. Of those that a mesh axis runs over, the one named last changes fastest.
Arguments:
- tokens: bfloat16 [32, 16, 128, 1152], P('dp', 'seq'), may hold values from -6 to 6
- norm_gains: float32 [2, 1152], replicated, may hold values from 0.1 to 1.9
- qkv_space: bfloat16 [1152, 1728], P(None, 'seq'), may hold values from -1 to 1
- out_space: bfloat16 [576, 1152], P(None, 'seq'), may hold values from -0.25 to 0.25
- qkv_time: bfloat16 [1152, 1728], P(None, 'seq'), may hold values from -1 to 1
- out_time: bfloat16 [576, 1152], P(None, 'seq'), may hold values from -0.25 to 0.25
- cotangent: bfloat16 [32, 16, 128, 1152], P('dp', None, 'seq'), may hold values from -6 to 6
Outputs:
- result: bfloat16 [32, 16, 128, 1152], P('dp', None, 'seq')
- d_tokens: bfloat16 [32, 16, 128, 1152], P('dp', 'seq')
- d_out_space: float32 [576, 1152], P(None, 'seq')
- d_out_time: float32 [576, 1152], P(None, 'seq')
- d_gains: float32 [2, 1152], P(None, 'seq')
The draws below stay inside these ranges and needn't reach their ends.
All inputs are finite; a program needn't handle non-finite values.
Results may differ from the reference program's by a relative error of at most 0.04.
Values may be sent and summed in bfloat16 or wider, within the bound.
A program may use at most 64 MiB of HBM per device.

```python
import jax
import jax.numpy as jnp
from jax import lax

D = 1152
HEADS = 8
HD = 72
P_SIZE = 128
F = 16
SAMPLES = 32
N_SEQ = 16


def projection(key):
    width = HEADS * HD
    base = jax.random.normal(key, (D, 3 * width), jnp.float32) * D ** (-0.5)
    queries = base[:, :width]
    keys_all = base[:, width:2 * width]
    return jnp.clip(jnp.concatenate([queries, keys_all, base[:, 2 * width:]], 1), -1.0, 1.0)


def draw_qkv_space(key, part):
    key = jax.random.fold_in(key, 5)
    return projection(key).astype(jnp.bfloat16)


def draw_qkv_time(key, part):
    key = jax.random.fold_in(key, 7)
    return projection(key).astype(jnp.bfloat16)


def raised(array, stream_key, source, target, shards_of, factor):
    owner, partner = [(jnp.arange(array.shape[axis_at]) // (array.shape[axis_at] // shards_of)).reshape([-1 if axis == axis_at else 1 for axis in range(array.ndim)]) for axis_at in (source, target)]
    chosen = jax.random.permutation(stream_key, shards_of)[partner]
    strong = (owner == chosen) | (owner == (partner + shards_of // 2) % shards_of)
    return jnp.where(strong, factor * array, array)


def block_levels(rng, dims, pieces, least, high):
    def one(position, shards_of):
        heights = jax.random.uniform(jax.random.fold_in(jax.random.fold_in(rng, 6), position), (shards_of,), jnp.float32, least / len(pieces), high / len(pieces))
        return jnp.repeat(jnp.exp(heights), dims[position] // shards_of).reshape((-1,) + (1,) * (len(dims) - position - 1))

    level = one(*pieces[0])
    for cut in pieces[1:]:
        level = level * one(*cut)
    return level


def scatter_about(stream_key, shape, spread, bound, cuts=(), dtype=jnp.bfloat16):
    drawn = jax.random.normal(stream_key, shape, jnp.float32) * spread
    if len(cuts) > 0:
        drawn = block_levels(stream_key, shape, cuts, -0.22, 0.18) * drawn
    return jnp.clip(drawn, min=-bound, max=bound).astype(dtype)


def heavy_noise(stream_key, shape, deviation, reach, pieces, heavy, kind=jnp.bfloat16):
    entries = deviation * jax.random.normal(stream_key, shape, jnp.float32)
    if pieces:
        entries = entries * block_levels(stream_key, shape, pieces, -0.22, 0.18)
    return jnp.clip(raised(entries, jax.random.fold_in(stream_key, 3), *heavy), -reach, reach).astype(kind)


def setup_inputs(seed: int = 0) -> dict:
    key_list = jax.random.split(jax.random.key(seed), 8)
    tokens = scatter_about(key_list[0], (SAMPLES, F, P_SIZE, D), 1.0, 6.0, ((0, 32), (1, 16)))
    norm_gains = jnp.clip(1.0 + 0.18 * jax.random.normal(key_list[1], (2, D), jnp.float32), 0.1, 1.9)
    qkv_space = draw_qkv_space(jax.random.fold_in(key_list[7], 71), 0)
    out_space = scatter_about(key_list[3], (HEADS * HD, D), (HEADS * HD) ** -0.5, 0.25, ((1, 16),))
    qkv_time = draw_qkv_time(jax.random.fold_in(key_list[7], 71), 0)
    out_time = scatter_about(key_list[5], (HEADS * HD, D), (HEADS * HD) ** -0.5, 0.25, ((1, 16),))
    cotangent = heavy_noise(key_list[6], (SAMPLES, F, P_SIZE, D), 1.0, 6.0, ((0, 32), (2, 16)), (2, 3, 16, 2.0))
    return dict(tokens=tokens, norm_gains=norm_gains, qkv_space=qkv_space, out_space=out_space, qkv_time=qkv_time, out_time=out_time, cotangent=cotangent)


norm_eps = 1e-06

def rounded(value):
    return lax.optimization_barrier(value.astype(jnp.bfloat16))

def matmul(left_side, right_side):
    rows = left_side.reshape(-1, left_side.shape[-1])
    product = jnp.dot(rows, right_side, preferred_element_type=jnp.float32)
    return product.reshape(left_side.shape[:-1] + (right_side.shape[-1],))

def norm_forward(hidden, gain):
    average = lax.optimization_barrier(jnp.mean(hidden, -1, keepdims=True))
    centered = hidden - average
    inv_std = lax.rsqrt(lax.optimization_barrier(jnp.mean(centered * centered, -1, keepdims=True)) + norm_eps)
    normed = centered * inv_std
    return (normed, inv_std, rounded(normed * gain))

def norm_backward(upstream, normed, inv_std, gain):
    scaled = upstream * gain
    return inv_std * (scaled - lax.optimization_barrier(jnp.mean(scaled, -1, keepdims=True)) - normed * lax.optimization_barrier(jnp.mean(scaled * normed, -1, keepdims=True)))

def split_heads(packed):
    leading = packed.shape[:-1]
    heads_all = packed.astype(jnp.float32).reshape(leading + (3, HEADS, HD))
    return (heads_all[..., 0, :, :], heads_all[..., 1, :, :], heads_all[..., 2, :, :])

def attend(packed):
    queries, keys_all, values_all = split_heads(packed)
    logits = jnp.einsum('...qhd,...khd->...hqk', queries, keys_all) * HD ** (-0.5)
    probs_all = jax.nn.softmax(logits, axis=-1)
    weights_b = rounded(probs_all)
    mixed = jnp.einsum('...hqk,...khd->...qhd', weights_b.astype(jnp.float32), values_all)
    return (probs_all, weights_b, rounded(mixed.reshape(packed.shape[:-1] + (HEADS * HD,))))

def attend_backward(packed, probs_all, weights_b, d_mixed):
    queries, keys_all, values_all = split_heads(packed)
    upstream = d_mixed.astype(jnp.float32).reshape(d_mixed.shape[:-1] + (HEADS, HD))
    d_weights = jnp.einsum('...qhd,...khd->...hqk', upstream, values_all)
    d_values = jnp.einsum('...hqk,...qhd->...khd', weights_b.astype(jnp.float32), upstream)
    d_logits = probs_all * (d_weights - lax.optimization_barrier(jnp.sum(d_weights * probs_all, -1, keepdims=True))) * HD ** (-0.5)
    d_logits = rounded(d_logits).astype(jnp.float32)
    d_queries = jnp.einsum('...hqk,...khd->...qhd', d_logits, keys_all)
    d_keys = jnp.einsum('...hqk,...qhd->...khd', d_logits, queries)
    stacked = jnp.stack([d_queries, d_keys, d_values], axis=-3)
    return rounded(stacked.reshape(packed.shape))

def reference(tokens, norm_gains, qkv_space, out_space, qkv_time, out_time, cotangent):
    blocks = P_SIZE // N_SEQ
    width = HEADS * HD

    def one_sample(pair):
        frames_in, cot_in = pair
        hidden = frames_in.astype(jnp.float32)
        normed_s, inv_s, xn_space = norm_forward(hidden, norm_gains[0])
        packed_space = rounded(matmul(xn_space, qkv_space))
        probs_space, weights_space, mixed_space = attend(packed_space)
        middle = rounded(hidden + matmul(mixed_space, out_space))
        middle_f = middle.transpose(1, 0, 2).astype(jnp.float32)
        normed_t, inv_t, xn_time = norm_forward(middle_f, norm_gains[1])
        packed_time = rounded(matmul(xn_time, qkv_time))
        probs_time, weights_time, mixed_time = attend(packed_time)
        result = rounded(middle_f + matmul(mixed_time, out_time))
        upstream = cot_in.transpose(1, 0, 2)
        d_mixed_time = rounded(matmul(upstream, out_time.T))
        d_packed_time = attend_backward(packed_time, probs_time, weights_time, d_mixed_time)
        d_xn_time = matmul(d_packed_time, qkv_time.T)
        d_middle = rounded(upstream.astype(jnp.float32) + norm_backward(d_xn_time, normed_t, inv_t, norm_gains[1]))
        d_middle_f = d_middle.transpose(1, 0, 2)
        d_mixed_space = rounded(matmul(d_middle_f, out_space.T))
        d_packed_space = attend_backward(packed_space, probs_space, weights_space, d_mixed_space)
        d_xn_space = matmul(d_packed_space, qkv_space.T)
        d_tokens = rounded(d_middle_f.astype(jnp.float32) + norm_backward(d_xn_space, normed_s, inv_s, norm_gains[0]))
        part_space = jnp.einsum('fph,fpd->fhd', mixed_space.astype(jnp.float32), d_middle_f.astype(jnp.float32))
        part_time = jnp.einsum('jph,jpd->jhd', mixed_time.reshape(N_SEQ, blocks * F, width).astype(jnp.float32), upstream.reshape(N_SEQ, blocks * F, D).astype(jnp.float32))
        sum_space = lax.optimization_barrier(jnp.sum(rounded(part_space).astype(jnp.float32), 0))
        sum_time = lax.optimization_barrier(jnp.sum(rounded(part_time).astype(jnp.float32), 0))
        gain_space = lax.optimization_barrier(jnp.sum(d_xn_space * normed_s, 1))
        gain_time = lax.optimization_barrier(jnp.sum((d_xn_time * normed_t).reshape(N_SEQ, blocks * F, D), 1))
        sum_gain = jnp.stack([lax.optimization_barrier(jnp.sum(rounded(gain_space).astype(jnp.float32), 0)), lax.optimization_barrier(jnp.sum(rounded(gain_time).astype(jnp.float32), 0))])
        return (result.transpose(1, 0, 2), d_tokens, sum_space, sum_time, sum_gain)
    result, d_tokens, sums_space, sums_time, sums_gain = lax.map(one_sample, (tokens, cotangent))
    return (result, d_tokens, lax.optimization_barrier(jnp.sum(sums_space, 0)), lax.optimization_barrier(jnp.sum(sums_time, 0)), lax.optimization_barrier(jnp.sum(sums_gain, 0)))
```

```python
import functools

import jax
import jax.numpy as jnp
from jax import lax
from jax.experimental import pallas as pl
from jax.experimental.pallas import tpu as pltpu
from jax.sharding import PartitionSpec as P

HEADS = 8
HD = 72
WIDTH = HEADS * HD
D = 1152
PARTS = 16
QC = 3 * WIDTH // PARTS
OC = D // PARTS
QR = 112
OR = 80
CHUNKS = ((0, QR), (QR, OR), (QR + OR, QR))
ROWS = 2 * QR + OR
TOK = 128
BLK = 384
QTR = 96
EPS = 1e-06
BF = jnp.bfloat16
F32 = jnp.float32
MESH = pl.DeviceIdType.MESH
NT = (((1,), (1,)), ((), ()))
NN = (((1,), (0,)), ((), ()))
TN = (((0,), (0,)), ((), ()))


def dot(left, right, dims):
    return lax.dot_general(left, right, dims, preferred_element_type=F32)


def rounded(value):
    return value.astype(BF).astype(F32)


def normalize(hidden):
    average = jnp.mean(hidden, -1, keepdims=True)
    centered = hidden - average
    inv_std = lax.rsqrt(jnp.mean(centered * centered, -1, keepdims=True) + EPS)
    return centered * inv_std, inv_std


def norm_backward(upstream, normed, inv_std, gain):
    scaled = upstream * gain
    return inv_std * (
        scaled
        - jnp.mean(scaled, -1, keepdims=True)
        - normed * jnp.mean(scaled * normed, -1, keepdims=True)
    )


def widened(column):
    return (column // QC) * QR + column % QC


def kernel(
    tokens, gains, pack, cot, result, d_tokens, d_space, d_time, d_gain,
    G, packed_s, packed_t, probs_s, probs_t, mixed_s, mixed_t, wide, flat, flat_x, d_mix,
    stack, send1, recv1, send2, recv2,
    B, R0, E, R1, FS, R2, H, R3, R4, Q, OUT, tmp,
    gsend, gplane, gcol, gall,
    loc, zr, xy1, xy2, sb, gs, gss, as_, ar, rs, rr, ps, pr,
):
    dp, seq = lax.axis_index("dp"), lax.axis_index("seq")
    x, y, z_hi = dp % 4, (dp // 4) % 4, dp // 16
    z, c = seq // 2, seq % 2
    Z = z_hi * 8 + z

    def at(x_, y_, Z_, c_):
        return ((Z_ // 8) * 16 + y_ * 4 + x_, (Z_ % 8) * 2 + c_)

    def copy(src, dst, ssem, rsem, device):
        pltpu.make_async_remote_copy(
            src_ref=src, dst_ref=dst, send_sem=ssem, recv_sem=rsem,
            device_id=device, device_id_type=MESH,
        ).start()

    def drain(ref, sem):
        pltpu.make_async_copy(ref, ref, sem).wait()

    def plane(n):
        other = (y * 4 + x + n) % 16
        return at(other % 4, other // 4, Z, c)

    def column(n):
        other = (Z * 2 + c + n) % 32
        return other, at(x, y, other // 2, other % 2)

    right, left = at(x, y, (Z + 1) % 16, c), at(x, y, (Z + 15) % 16, c)
    sibling = at(x, y, Z, 1 - c)
    xp, xm = at((x + 1) % 4, y, Z, c), at((x + 3) % 4, y, Z, c)
    yp, ym = at(x, (y + 1) % 4, Z, c), at(x, (y + 3) % 4, Z, c)

    barrier = pltpu.get_barrier_semaphore()

    def greet_plane(n, carry):
        pl.semaphore_signal(barrier, inc=1, device_id=plane(n), device_id_type=MESH)
        return carry

    def greet_column(n, carry):
        pl.semaphore_signal(barrier, inc=1, device_id=column(n)[1], device_id_type=MESH)
        return carry

    lax.fori_loop(1, 16, greet_plane, 0)
    lax.fori_loop(1, 32, greet_column, 0)
    own = pltpu.make_async_copy(pack, G.at[z, c], loc)
    own.start()
    own.wait()
    pl.semaphore_wait(barrier, 46)

    units = (x, 4 + y, 8)

    def tile(zs, k, u):
        r0, n = CHUNKS[k]
        return G.at[zs, c, pl.ds(r0, n), pl.ds(pl.multiple_of(u * 128, 128), 128)]

    def lanes(k, n):
        r0, rows = CHUNKS[k]
        return G.at[0, 0, pl.ds(r0, rows), pl.ds(0, 128 * n)]

    def shards(k, n):
        r0, rows = CHUNKS[k]
        return G.at[pl.ds(0, n), 0, pl.ds(r0, rows), :]

    def whole(zs, k):
        r0, rows = CHUNKS[k]
        return G.at[zs, c, pl.ds(r0, rows), :]

    def hand_on(zs, k, u, rsem, device):
        copy(tile(zs, k, u), tile(zs, k, u), gs.at[k], rsem, device)

    def to_sibling(zs, k, h):
        copy(whole(zs, k), whole(zs, k), gss.at[k], sb.at[k, h], sibling)

    def begin(k):
        for u in units:
            hand_on(z, k, u, zr.at[k, 0, 0], right)
            hand_on(z, k, u, zr.at[k, 1, 0], left)
        to_sibling(z, k, 0)

    def from_z(k, h):
        zl, zq = (z + 8 - h) % 8, (z + h) % 8
        if h < 4:
            drain(lanes(k, 3), zr.at[k, 0, h - 1])
            for u in units if h < 3 else (units[1:] if k % 2 else units[1:2]):
                hand_on(zl, k, u, zr.at[k, 0, h], right)
            drain(lanes(k, 3), zr.at[k, 1, h - 1])
            for u in units if h < 3 else (units[:1] if k % 2 else units[::2]):
                hand_on(zq, k, u, zr.at[k, 1, h], left)
        else:
            drain(lanes(k, 2 if k % 2 else 1), zr.at[k, 0, 3])
            drain(lanes(k, 1 if k % 2 else 2), zr.at[k, 1, 3])
        for zs in (zl, zq) if h < 4 else (zl,):
            hand_on(zs, k, x, xy1.at[k, h - 1], xp)
            hand_on(zs, k, x, xy1.at[k, h - 1], xm)
            hand_on(zs, k, 4 + y, xy1.at[k, h - 1], yp)
            hand_on(zs, k, 4 + y, xy1.at[k, h - 1], ym)

    def from_plane(k, h):
        zl, zq = (z + 8 - h) % 8, (z + h) % 8
        drain(lanes(k, 8 if h < 4 else 4), xy1.at[k, h - 1])
        hand_on(zl, k, (x + 3) % 4, xy2.at[k, h - 1], xp)
        if h < 4:
            hand_on(zl, k, 4 + (y + 3) % 4, xy2.at[k, h - 1], yp)
            hand_on(zq, k, (x + 1) % 4, xy2.at[k, h - 1], xm)
        hand_on(zq, k, 4 + (y + 1) % 4, xy2.at[k, h - 1], ym)

    def last_of_plane(k, h):
        zl, zq = (z + 8 - h) % 8, (z + h) % 8
        drain(lanes(k, 4 if h < 4 else 2), xy2.at[k, h - 1])
        for zs in (zl, zq) if h < 4 else (zl,):
            to_sibling(zs, k, h)

    events = []
    for k in range(3):
        base = 2.0 * k
        events.append((base - 0.1, k, functools.partial(begin, k)))
        for h in range(1, 5):
            events.append((base + h, k, functools.partial(from_z, k, h)))
            events.append((base + h + 1.15, k, functools.partial(from_plane, k, h)))
            events.append((base + h + 2.3, k, functools.partial(last_of_plane, k, h)))
    events.sort(key=lambda event: event[0])

    def pump(n):
        for _ in range(min(n, len(events))):
            events.pop(0)[2]()

    def need(k):
        while any(event[1] == k for event in events):
            pump(1)
        for h in range(5):
            drain(shards(k, 2 if 0 < h < 4 else 1), sb.at[k, h])

    def project(k, xn, packed):
        r0 = CHUNKS[k][0]
        for j in range(8):
            part = rounded(dot(G[j, :, r0:r0 + QR, :].reshape(2 * QR, D), xn, NT))
            packed[2 * QC * j:2 * QC * j + QC, :] = part[:QC]
            packed[2 * QC * j + QC:2 * QC * (j + 1), :] = part[QR:QR + QC]

    def heads_of(packed, h):
        return tuple(
            packed[i * WIDTH + HD * h:i * WIDTH + HD * (h + 1), :].astype(BF) for i in range(3)
        )

    def attend(packed, probs, mixed, start, mask, between):
        for h in range(HEADS):
            q, k, v = heads_of(packed, h)
            logits = dot(k, q, TN) * HD ** (-0.5)
            if mask is not None:
                logits = jnp.where(mask, logits, -1e30)
            raised = jnp.exp(logits - jnp.max(logits, 0, keepdims=True))
            p = raised / jnp.sum(raised, 0, keepdims=True)
            probs[h] = p
            mixed[start + HD * h:start + HD * (h + 1), :] = rounded(dot(v, p.astype(BF), NN))
            between()

    def project_out(mixed):
        m = mixed[0:D, :].astype(BF)
        for j in range(8):
            part = dot(G[j, :, QR:QR + OR, :].reshape(2 * OR, D), m, NN)
            flat[2 * OC * j:2 * OC * j + OC, :] = part[:OC]
            flat[2 * OC * j + OC:2 * OC * (j + 1), :] = part[OR:OR + OC]
        return flat[...].T

    def project_out_back(upstream, first, start):
        turned = upstream.T
        flat[...] = turned
        for j in range(PARTS):
            flat_x[OR * j:OR * j + OC, :] = flat[OC * j:OC * (j + 1), :]
            flat_x[OR * j + OC:OR * (j + 1), :] = jnp.zeros((OR - OC, TOK), F32)
        across = flat_x[...].T.astype(BF)
        total = jnp.zeros((TOK, 640), F32)
        for j in range(2):
            w = G[4 * j:4 * j + 4, :, QR:QR + OR, first:first + 640].reshape(8 * OR, 640)
            total += dot(across[:, 8 * OR * j:8 * OR * (j + 1)], w, NN)
        d_mix[...] = rounded(total.T[start:start + WIDTH])

    def outer(mixed, start, blocks):
        m = mixed[start:start + 640, :].astype(BF)
        tmp[360:BLK, :] = jnp.zeros((BLK - 360, 128), F32)
        for j in range(4):
            part = dot(flat[4 * OC * j:4 * OC * (j + 1), :].astype(BF), m, NT)
            for i in range(4):
                for t in range(5):
                    tmp[OC * t:OC * (t + 1), :] = part[OC * i:OC * (i + 1), 128 * t:128 * (t + 1)]
                blocks[2 * j + i // 2, i % 2] = tmp[...].astype(BF)

    def attend_back(packed, probs, between):
        for j in range(PARTS):
            wide[QR * j + QC:QR * (j + 1), :] = jnp.zeros((QR - QC, TOK), F32)
        for h in range(HEADS):
            q, k, v = heads_of(packed, h)
            dm = d_mix[HD * h:HD * (h + 1), :].astype(BF)
            p = probs[h]
            d_w = dot(v, dm, TN)
            d_v = dot(dm, p.astype(BF), NT)
            d_s = (p * (d_w - jnp.sum(d_w * p, 0, keepdims=True)) * HD ** (-0.5)).astype(BF)
            for i, part in enumerate((dot(k, d_s, NN), dot(q, d_s, NT), d_v)):
                col = i * WIDTH + HD * h
                if widened(col + 36) == widened(col) + 36:
                    wide[widened(col):widened(col) + HD, :] = part
                else:
                    wide[widened(col):widened(col) + 36, :] = part[:36]
                    wide[widened(col + 36):widened(col + 36) + 36, :] = part[36:]
            between()

    def project_back(k):
        r0 = CHUNKS[k][0]
        across = wide[...].T.astype(BF)
        total = jnp.zeros((TOK, D), F32)
        for j in range(2):
            w = G[4 * j:4 * j + 4, :, r0:r0 + QR, :].reshape(8 * QR, D)
            total += dot(across[:, 8 * QR * j:8 * QR * (j + 1)], w, NN)
        return total

    def exchange_start(src, dst, i):
        def step(n, carry):
            t = (seq + n) % PARTS
            copy(src.at[t], dst.at[seq], as_.at[i], ar.at[i], (dp, t))
            return carry

        lax.fori_loop(1, PARTS, step, 0)
        dst[seq] = src[seq]

    def exchange_done(dst, i):
        drain(dst.at[pl.ds(0, PARTS - 1)], ar.at[i])

    def reduce0(t):
        copy(B.at[t, :, 1 - c], R0.at[t], rs.at[t, 0], rr.at[t, 0], sibling)

    def reduce1(t):
        drain(R0.at[t], rr.at[t, 0])
        for i in range(8):
            E[t, i // 2, i % 2] = (B[t, i, c].astype(F32) + R0[t, i].astype(F32)).astype(BF)
        for d in range(1, 4):
            xd, yd = (x + d) % 4, (y + d) % 4
            rows = pl.ds(pl.multiple_of(QTR * xd, 16), QTR)
            copy(E.at[t, :, 0, rows], R1.at[t, 0, d - 1], rs.at[t, 1], rr.at[t, 1], at(xd, y, Z, c))
            rows = pl.ds(pl.multiple_of(QTR * yd, 16), QTR)
            copy(E.at[t, :, 1, rows], R1.at[t, 1, d - 1], rs.at[t, 1], rr.at[t, 1], at(x, yd, Z, c))

    def reduce2(t):
        drain(R1.at[t], rr.at[t, 1])
        for side, at_ in enumerate((x, y)):
            rows = pl.ds(pl.multiple_of(QTR * at_, 16), QTR)
            for i in range(4):
                total = E[t, i, side, rows, :].astype(F32)
                for d in range(3):
                    total += R1[t, side, d, i].astype(F32)
                FS[t, side, i] = total.astype(BF)
        for d in range(1, 4):
            xd, yd = (x + d) % 4, (y + d) % 4
            copy(FS.at[t, 0, yd], R2.at[t, 0, d - 1], rs.at[t, 2], rr.at[t, 2], at(x, yd, Z, c))
            copy(FS.at[t, 1, xd], R2.at[t, 1, d - 1], rs.at[t, 2], rr.at[t, 2], at(xd, y, Z, c))

    owner_a = jnp.logical_and(z % 2 == 0, y == z // 2)
    owner_b = jnp.logical_and(z % 2 == 1, x == z // 2)
    owner = jnp.logical_or(owner_a, owner_b)
    homes = (2 * y, 2 * x + 1)
    pos = [(Z - home + 3 + 16) % 16 for home in homes]

    def reduce3(t):
        drain(R2.at[t], rr.at[t, 2])
        for side, at_ in enumerate((y, x)):
            total = FS[t, side, at_].astype(F32)
            for d in range(3):
                total += R2[t, side, d].astype(F32)
            H[t, side] = total.astype(BF)
        for side in range(2):
            home = homes[side] + 8 * (pos[side] // 8)

            @pl.when(home != Z)
            def _():
                copy(
                    H.at[t, side], R3.at[t, pos[side] % 8], rs.at[t, 3 + side], rr.at[t, 3],
                    at(x, y, home, c),
                )

            @pl.when(home == Z)
            def _():
                R3[t, 3] = H[t, side]

    def reduce4(t):
        @pl.when(owner)
        def _():
            drain(R3.at[t, pl.ds(0, 7)], rr.at[t, 3])
            total = R3[t, 0].astype(F32)
            for i in range(1, 8):
                total += R3[t, i].astype(F32)
            Q[t, 0] = total.astype(BF)
            copy(
                Q.at[t, 0], R4.at[t], rs.at[t, 5], rr.at[t, 4], at(x, y, (Z + 8) % 16, c)
            )

    quarter = pl.ds(pl.multiple_of(QTR * jnp.where(z % 2 == 0, x, y), 16), QTR)

    def reduce5(t):
        @pl.when(owner)
        def _():
            drain(R4.at[t], rr.at[t, 4])
            total = (Q[t, 0].astype(F32) + R4[t].astype(F32)).astype(BF)
            Q[t, 1] = total
            OUT[t, quarter, :] = total

            def step(n, carry):
                copy(Q.at[t, 1], OUT.at[t, quarter, :], rs.at[t, 6], rr.at[t, 5], plane(n))
                return carry

            lax.fori_loop(1, 16, step, 0)

    def reduce6(t, out):
        @pl.when(owner)
        def _():
            drain(OUT.at[t, pl.ds(0, 3 * QTR)], rr.at[t, 5])

        @pl.when(jnp.logical_not(owner))
        def _():
            drain(OUT.at[t], rr.at[t, 5])

        tmp[...] = OUT[t].astype(F32)
        for i in range(5):
            n = min(128, WIDTH - 128 * i)
            out[128 * i:128 * i + n, :] = tmp[OC * i:OC * (i + 1), :].T[:n]

    def reduce_sent(t):
        drain(R0.at[t], rs.at[t, 0])
        drain(R1.at[t], rs.at[t, 1])
        drain(R2.at[t], rs.at[t, 2])
        for side in range(2):
            home = homes[side] + 8 * (pos[side] // 8)

            @pl.when(home != Z)
            def _():
                drain(H.at[t, side], rs.at[t, 3 + side])

        @pl.when(owner)
        def _():
            drain(Q.at[t, 0], rs.at[t, 5])
            drain(gauge.at[pl.ds(0, 15)], rs.at[t, 6])

    gauge = stack

    mixed_s[WIDTH:, :] = jnp.zeros((mixed_s.shape[0] - WIDTH, TOK), F32)
    mixed_t[:WIDTH, :] = jnp.zeros((WIDTH, TOK), F32)
    mixed_t[D:, :] = jnp.zeros((mixed_t.shape[0] - D, TOK), F32)
    hidden = tokens[...].astype(F32)
    xn = (normalize(hidden)[0] * gains[0:1, :]).astype(BF)
    need(0)
    project(0, xn, packed_s)
    pump(1)
    attend(packed_s, probs_s, mixed_s, 0, None, lambda: pump(1))
    need(1)
    middle = tokens[...].astype(F32) + project_out(mixed_s)
    send1[...] = middle.reshape(PARTS, 8, D).astype(BF)
    exchange_start(send1, recv1, 0)

    upstream = cot[...].astype(F32).reshape(TOK, D)
    project_out_back(upstream, 512, 64)
    need(2)
    exchange_done(recv1, 0)
    middle_t = recv1[...].astype(F32).reshape(TOK, D)
    normed, inv_std = normalize(middle_t)
    project(2, (normed * gains[1:2, :]).astype(BF), packed_t)
    mask = lax.broadcasted_iota(jnp.int32, (TOK, TOK), 0) % 8 == (
        lax.broadcasted_iota(jnp.int32, (TOK, TOK), 1) % 8
    )
    attend(packed_t, probs_t, mixed_t, WIDTH, mask, lambda: None)
    attend_back(packed_t, probs_t, lambda: None)
    d_xn = project_back(2)
    middle_t = recv1[...].astype(F32).reshape(TOK, D)
    normed, inv_std = normalize(middle_t)
    gain_time = jnp.sum(d_xn * normed, 0, keepdims=True)
    d_middle = cot[...].astype(F32).reshape(TOK, D) + norm_backward(
        d_xn, normed, inv_std, gains[1:2, :]
    )
    send2[...] = d_middle.reshape(PARTS, 8, D).astype(BF)
    exchange_start(send2, recv2, 1)
    outer(mixed_t, WIDTH, B.at[0])
    reduce0(0)
    out_t = project_out(mixed_t)
    result[...] = (recv1[...].astype(F32) + out_t.reshape(PARTS, 8, D)).astype(BF)
    reduce1(0)

    exchange_done(recv2, 1)
    frame = recv2[...].astype(F32).reshape(TOK, D)
    project_out_back(frame, 0, 0)
    outer(mixed_s, 0, B.at[1])
    reduce0(1)
    reduce2(0)
    reduce1(1)
    reduce3(0)
    turns = [
        lambda: None, lambda: reduce2(1), lambda: reduce4(0), lambda: None,
        lambda: reduce3(1), lambda: reduce5(0), lambda: None, lambda: reduce4(1),
    ]
    attend_back(packed_s, probs_s, lambda: turns.pop(0)())
    reduce5(1)
    d_xn = project_back(0)
    normed, inv_std = normalize(tokens[...].astype(F32))
    gain_space = jnp.sum(d_xn * normed, 0, keepdims=True)

    gsend[...] = jnp.zeros(gsend.shape, F32)
    for j in range(PARTS):
        gsend[j:j + 1, 0:OC] = gain_space[:, OC * j:OC * (j + 1)]
        gsend[j:j + 1, 128:128 + OC] = gain_time[:, OC * j:OC * (j + 1)]
    mine = y * 4 + x
    gplane[mine] = gsend[...].astype(BF)

    def to_plane(n, carry):
        copy(gplane.at[mine], gplane.at[mine], ps.at[0], pr.at[0], plane(n))
        return carry

    lax.fori_loop(1, 16, to_plane, 0)
    d_tokens[...] = (
        recv2[...].astype(F32).reshape(TOK, D)
        + norm_backward(d_xn, normed, inv_std, gains[0:1, :])
    ).astype(BF)
    drain(gplane.at[pl.ds(0, 15)], pr.at[0])
    total = gplane[0].astype(F32)
    for i in range(1, 16):
        total += gplane[i].astype(F32)
    for j in range(PARTS):
        gcol[j] = total[j:j + 1]
    me = Z * 2 + c

    def to_column(n, carry):
        other, device = column(n)
        copy(gcol.at[other % 16], gall.at[me], ps.at[1], pr.at[1], device)
        return carry

    lax.fori_loop(1, 32, to_column, 0)
    gall[me] = gcol[me % 16]
    reduce6(0, d_time)
    reduce6(1, d_space)
    drain(gall.at[pl.ds(0, 31)], pr.at[1])
    total = gall[0]
    for i in range(1, 32):
        total += gall[i]
    d_gain[0:1, :] = total[:, 0:OC]
    d_gain[1:2, :] = total[:, 128:128 + OC]

    for k in range(3):
        drain(shards(k, 7), gs.at[k])
        drain(shards(k, 8), gss.at[k])
    drain(send1.at[pl.ds(0, 15)], as_.at[0])
    drain(send2.at[pl.ds(0, 15)], as_.at[1])
    reduce_sent(0)
    reduce_sent(1)
    drain(gplane.at[pl.ds(0, 15)], ps.at[0])
    drain(gall.at[pl.ds(0, 31)], ps.at[1])


def local(tokens, norm_gains, qkv_space, out_space, qkv_time, out_time, cotangent):
    pad = lambda a, n: jnp.pad(a, ((0, n - a.shape[0]), (0, 0)))
    pack = jnp.concatenate(
        [
            pad(qkv_space.T, QR),
            pad(jnp.concatenate([out_space.T, out_time.T], 1), OR),
            pad(qkv_time.T, QR),
        ],
        0,
    )
    vmem, sem = pltpu.VMEM, pltpu.SemaphoreType.DMA
    any_spec = pl.BlockSpec(memory_space=pl.ANY)
    in_vmem = pl.BlockSpec(memory_space=pltpu.VMEM)
    result, d_tokens, d_space, d_time, d_gain = pl.pallas_call(
        kernel,
        out_shape=(
            jax.ShapeDtypeStruct((16, 8, D), BF),
            jax.ShapeDtypeStruct((TOK, D), BF),
            jax.ShapeDtypeStruct((WIDTH, OC), F32),
            jax.ShapeDtypeStruct((WIDTH, OC), F32),
            jax.ShapeDtypeStruct((2, OC), F32),
        ),
        in_specs=[in_vmem, in_vmem, any_spec, in_vmem],
        out_specs=(in_vmem,) * 5,
        scratch_shapes=[
            vmem((8, 2, ROWS, D), BF),
            vmem((3 * WIDTH, TOK), F32),
            vmem((3 * WIDTH, TOK), F32),
            vmem((HEADS, TOK, TOK), F32),
            vmem((HEADS, TOK, TOK), F32),
            vmem((D + 64, TOK), F32),
            vmem((D + 64, TOK), F32),
            vmem((PARTS * QR, TOK), F32),
            vmem((D, TOK), F32),
            vmem((PARTS * OR, TOK), F32),
            vmem((WIDTH, TOK), F32),
            vmem((16, QTR, 128), BF),
            vmem((PARTS, 8, D), BF),
            vmem((PARTS, 8, D), BF),
            vmem((PARTS, 8, D), BF),
            vmem((PARTS, 8, D), BF),
            vmem((2, 8, 2, BLK, 128), BF),
            vmem((2, 8, BLK, 128), BF),
            vmem((2, 4, 2, BLK, 128), BF),
            vmem((2, 2, 3, 4, QTR, 128), BF),
            vmem((2, 2, 4, QTR, 128), BF),
            vmem((2, 2, 3, QTR, 128), BF),
            vmem((2, 2, QTR, 128), BF),
            vmem((2, 8, QTR, 128), BF),
            vmem((2, QTR, 128), BF),
            vmem((2, 2, QTR, 128), BF),
            vmem((2, BLK, 128), BF),
            vmem((BLK, 128), F32),
            vmem((16, 256), F32),
            vmem((16, 16, 256), BF),
            vmem((16, 1, 256), F32),
            vmem((32, 1, 256), F32),
            sem,
            sem((3, 2, 4)),
            sem((3, 4)),
            sem((3, 4)),
            sem((3, 5)),
            sem((3,)),
            sem((3,)),
            sem((2,)),
            sem((2,)),
            sem((2, 7)),
            sem((2, 6)),
            sem((2,)),
            sem((2,)),
        ],
        compiler_params=pltpu.CompilerParams(
            collective_id=0, has_side_effects=True, vmem_limit_bytes=56 * 1024 * 1024
        ),
        name="block_pair",
    )(tokens.reshape(TOK, D), norm_gains, pack, cotangent.reshape(16, 8, D))
    return (
        result.reshape(1, 16, 8, D),
        d_tokens.reshape(1, 1, TOK, D),
        d_space,
        d_time,
        d_gain,
    )


def solution(mesh):
    return jax.shard_map(
        local,
        mesh=mesh,
        in_specs=(
            P("dp", "seq", None, None),
            P(),
            P(None, "seq"),
            P(None, "seq"),
            P(None, "seq"),
            P(None, "seq"),
            P("dp", None, "seq", None),
        ),
        out_specs=(
            P("dp", None, "seq", None),
            P("dp", "seq", None, None),
            P(None, "seq"),
            P(None, "seq"),
            P(None, "seq"),
        ),
        check_vma=False,
    )
```

```python
import functools

import jax
import jax.numpy as jnp
from jax import lax
from jax.experimental import pallas as pl
from jax.experimental.pallas import tpu as pltpu
from jax.sharding import PartitionSpec as P

HEADS = 8
HD = 72
WIDTH = HEADS * HD
D = 1152
PARTS = 16
QC = 3 * WIDTH // PARTS
OC = D // PARTS
QR = 112
OR = 80
CHUNKS = ((0, QR), (QR, OR), (QR + OR, QR))
ROWS = 2 * QR + OR
TOK = 128
BLK = 384
QTR = 96
SUB = 48
EPS = 1e-06
BF = jnp.bfloat16
F32 = jnp.float32
MESH = pl.DeviceIdType.MESH
NT = (((1,), (1,)), ((), ()))
NN = (((1,), (0,)), ((), ()))
TN = (((0,), (0,)), ((), ()))


def dot(left, right, dims):
    return lax.dot_general(left, right, dims, preferred_element_type=F32)


def rounded(value):
    return value.astype(BF).astype(F32)


def normalize(hidden):
    average = jnp.mean(hidden, -1, keepdims=True)
    centered = hidden - average
    inv_std = lax.rsqrt(jnp.mean(centered * centered, -1, keepdims=True) + EPS)
    return centered * inv_std, inv_std


def norm_backward(upstream, normed, inv_std, gain):
    scaled = upstream * gain
    return inv_std * (
        scaled
        - jnp.mean(scaled, -1, keepdims=True)
        - normed * jnp.mean(scaled * normed, -1, keepdims=True)
    )


def widened(column):
    return (column // QC) * QR + column % QC


def kernel(
    tokens_in, gains, qkv_s_in, out_s_in, qkv_t_in, out_t_in, cot_in,
    result, d_tokens, d_space, d_time, d_gain,
    tokens, qkv_s, out_s, qkv_t, out_t, cot,
    G, packed_s, packed_t, probs_s, probs_t, mixed_s, mixed_t, mixed_p, wide, flat, flat_x, d_mix,
    send1, recv1, send2, recv2, send3, recv3,
    B, R0, E, R1, FS, R2, H, R3, Q, R4, OUT, tmp,
    gsend, gplane, gcol, gall,
    loads, zr, xy1, xy2, sb, gs, gss, as_, ar, rs, rr, ps, pr,
):
    dp, seq = lax.axis_index("dp"), lax.axis_index("seq")
    x, y, z_hi = dp % 4, (dp // 4) % 4, dp // 16
    z, c = seq // 2, seq % 2
    Z = z_hi * 8 + z

    def at(x_, y_, Z_, c_):
        return ((Z_ // 8) * 16 + y_ * 4 + x_, (Z_ % 8) * 2 + c_)

    def copy(src, dst, ssem, rsem, device):
        pltpu.make_async_remote_copy(
            src_ref=src, dst_ref=dst, send_sem=ssem, recv_sem=rsem,
            device_id=device, device_id_type=MESH,
        ).start()

    def drain(ref, sem):
        pltpu.make_async_copy(ref, ref, sem).wait()

    def plane(n):
        other = (y * 4 + x + n) % 16
        return at(other % 4, other // 4, Z, c)

    def column(n):
        other = (Z * 2 + c + n) % 32
        return other, at(x, y, other // 2, other % 2)

    right, left = at(x, y, (Z + 1) % 16, c), at(x, y, (Z + 15) % 16, c)
    sibling = at(x, y, Z, 1 - c)
    xp, xm = at((x + 1) % 4, y, Z, c), at((x + 3) % 4, y, Z, c)
    yp, ym = at(x, (y + 1) % 4, Z, c), at(x, (y + 3) % 4, Z, c)

    barrier = pltpu.get_barrier_semaphore()

    def greet(device):
        pl.semaphore_signal(barrier, inc=1, device_id=device, device_id_type=MESH)

    def greet_column(n, carry):
        greet(column(n)[1])
        greet(column(32 - n)[1])
        return carry

    def greet_plane(n, carry):
        greet(plane(n))
        greet(plane(16 - n))
        return carry

    lax.fori_loop(1, 5, greet_column, 0)
    lax.fori_loop(1, 8, greet_plane, 0)
    greet(plane(8))
    lax.fori_loop(5, 16, greet_column, 0)
    greet(column(16)[1])

    arrays = (
        (qkv_s_in, qkv_s), (tokens_in, tokens), (out_s_in, out_s), (out_t_in, out_t),
        (qkv_t_in, qkv_t), (cot_in, cot),
    )
    loading = [
        pltpu.make_async_copy(src, dst, loads.at[i]) for i, (src, dst) in enumerate(arrays)
    ]
    for load in loading:
        load.start()

    def own_columns(k, ref):
        r0, n = CHUNKS[k]
        G[z, c, r0:r0 + n, :] = jnp.concatenate(
            [ref[...].astype(F32), jnp.zeros((QR - QC, D), F32)], 0
        ).astype(BF)

    loading[0].wait()
    own_columns(0, qkv_s)
    pl.semaphore_wait(barrier, 46)

    units = (x, 4 + y, 8)

    def tile(zs, k, u):
        r0, n = CHUNKS[k]
        return G.at[zs, c, pl.ds(r0, n), pl.ds(pl.multiple_of(u * 128, 128), 128)]

    def lanes(k, n):
        r0, rows = CHUNKS[k]
        return G.at[0, 0, pl.ds(r0, rows), pl.ds(0, 128 * n)]

    def shards(k, n):
        r0, rows = CHUNKS[k]
        return G.at[pl.ds(0, n), 0, pl.ds(r0, rows), :]

    def whole(zs, k):
        r0, rows = CHUNKS[k]
        return G.at[zs, c, pl.ds(r0, rows), :]

    def hand_on(zs, k, u, rsem, device):
        copy(tile(zs, k, u), tile(zs, k, u), gs.at[k], rsem, device)

    def to_sibling(zs, k, h):
        copy(whole(zs, k), whole(zs, k), gss.at[k], sb.at[k, h], sibling)

    def begin(k):
        for u in units:
            hand_on(z, k, u, zr.at[k, 0, 0], right)
            hand_on(z, k, u, zr.at[k, 1, 0], left)
        to_sibling(z, k, 0)

    def from_z(k, h):
        zl, zq = (z + 8 - h) % 8, (z + h) % 8
        if h < 4:
            drain(lanes(k, 3), zr.at[k, 0, h - 1])
            for u in units if h < 3 else (units[1:] if k % 2 else units[1:2]):
                hand_on(zl, k, u, zr.at[k, 0, h], right)
            drain(lanes(k, 3), zr.at[k, 1, h - 1])
            for u in units if h < 3 else (units[:1] if k % 2 else units[::2]):
                hand_on(zq, k, u, zr.at[k, 1, h], left)
        else:
            drain(lanes(k, 2 if k % 2 else 1), zr.at[k, 0, 3])
            drain(lanes(k, 1 if k % 2 else 2), zr.at[k, 1, 3])
        for zs in (zl, zq) if h < 4 else (zl,):
            hand_on(zs, k, x, xy1.at[k, h - 1], xp)
            hand_on(zs, k, x, xy1.at[k, h - 1], xm)
            hand_on(zs, k, 4 + y, xy1.at[k, h - 1], yp)
            hand_on(zs, k, 4 + y, xy1.at[k, h - 1], ym)

    def from_plane(k, h):
        zl, zq = (z + 8 - h) % 8, (z + h) % 8
        drain(lanes(k, 8 if h < 4 else 4), xy1.at[k, h - 1])
        hand_on(zl, k, (x + 3) % 4, xy2.at[k, h - 1], xp)
        if h < 4:
            hand_on(zl, k, 4 + (y + 3) % 4, xy2.at[k, h - 1], yp)
            hand_on(zq, k, (x + 1) % 4, xy2.at[k, h - 1], xm)
        hand_on(zq, k, 4 + (y + 1) % 4, xy2.at[k, h - 1], ym)

    def last_of_plane(k, h):
        zl, zq = (z + 8 - h) % 8, (z + h) % 8
        drain(lanes(k, 4 if h < 4 else 2), xy2.at[k, h - 1])
        for zs in (zl, zq) if h < 4 else (zl,):
            to_sibling(zs, k, h)

    events = []
    for k in range(3):
        base = 2.0 * k
        events.append((base - 0.1, k, functools.partial(begin, k)))
        for h in range(1, 5):
            events.append((base + h, k, functools.partial(from_z, k, h)))
            events.append((base + h + 1.15, k, functools.partial(from_plane, k, h)))
            events.append((base + h + 2.3, k, functools.partial(last_of_plane, k, h)))
    events.sort(key=lambda event: event[0])

    def pump(n):
        for _ in range(min(n, len(events))):
            events.pop(0)[2]()

    def need(k):
        while any(event[1] == k for event in events):
            pump(1)
        for h in range(5):
            drain(shards(k, 2 if 0 < h < 4 else 1), sb.at[k, h])

    def project(k, xn, packed):
        r0 = CHUNKS[k][0]
        for j in range(8):
            part = rounded(dot(G[j, :, r0:r0 + QR, :].reshape(2 * QR, D), xn, NT))
            packed[2 * QC * j:2 * QC * j + QC, :] = part[:QC]
            packed[2 * QC * j + QC:2 * QC * (j + 1), :] = part[QR:QR + QC]

    def heads_of(packed, h):
        return tuple(
            packed[i * WIDTH + HD * h:i * WIDTH + HD * (h + 1), :].astype(BF) for i in range(3)
        )

    def attend(packed, probs, mixed, start, mask, between):
        for h in range(HEADS):
            q, k, v = heads_of(packed, h)
            logits = dot(k, q, TN) * HD ** (-0.5)
            if mask is not None:
                logits = jnp.where(mask, logits, -1e30)
            raised = jnp.exp(logits - jnp.max(logits, 0, keepdims=True))
            p = raised / jnp.sum(raised, 0, keepdims=True)
            probs[h] = p
            mixed[start + HD * h:start + HD * (h + 1), :] = rounded(dot(v, p.astype(BF), NN))
            between()

    def project_out(mixed):
        m = mixed[0:D, :].astype(BF)
        for j in range(8):
            part = dot(G[j, :, QR:QR + OR, :].reshape(2 * OR, D), m, NN)
            flat[2 * OC * j:2 * OC * j + OC, :] = part[:OC]
            flat[2 * OC * j + OC:2 * OC * (j + 1), :] = part[OR:OR + OC]
        return flat[...].T

    def project_out_back(upstream, first, start):
        flat[...] = upstream.T
        for j in range(PARTS):
            flat_x[OR * j:OR * j + OC, :] = flat[OC * j:OC * (j + 1), :]
            flat_x[OR * j + OC:OR * (j + 1), :] = jnp.zeros((OR - OC, TOK), F32)
        across = flat_x[...].T.astype(BF)
        total = jnp.zeros((TOK, 640), F32)
        for j in range(2):
            w = G[4 * j:4 * j + 4, :, QR:QR + OR, first:first + 640].reshape(8 * OR, 640)
            total += dot(across[:, 8 * OR * j:8 * OR * (j + 1)], w, NN)
        d_mix[...] = rounded(total.T[start:start + WIDTH])

    def outer(mixed, start, blocks):
        m = mixed[start:start + 640, :].astype(BF)
        tmp[360:BLK, :] = jnp.zeros((BLK - 360, 128), F32)
        for j in range(4):
            part = dot(flat[4 * OC * j:4 * OC * (j + 1), :].astype(BF), m, NT)
            for i in range(4):
                for t in range(5):
                    tmp[OC * t:OC * (t + 1), :] = part[OC * i:OC * (i + 1), 128 * t:128 * (t + 1)]
                blocks[2 * j + i // 2, i % 2] = tmp[...].astype(BF)

    def attend_back(packed, probs, between):
        for j in range(PARTS):
            wide[QR * j + QC:QR * (j + 1), :] = jnp.zeros((QR - QC, TOK), F32)
        for h in range(HEADS):
            q, k, v = heads_of(packed, h)
            dm = d_mix[HD * h:HD * (h + 1), :].astype(BF)
            p = probs[h]
            d_w = dot(v, dm, TN)
            d_v = dot(dm, p.astype(BF), NT)
            d_s = (p * (d_w - jnp.sum(d_w * p, 0, keepdims=True)) * HD ** (-0.5)).astype(BF)
            for i, part in enumerate((dot(k, d_s, NN), dot(q, d_s, NT), d_v)):
                col = i * WIDTH + HD * h
                if widened(col + 36) == widened(col) + 36:
                    wide[widened(col):widened(col) + HD, :] = part
                else:
                    wide[widened(col):widened(col) + 36, :] = part[:36]
                    wide[widened(col + 36):widened(col + 36) + 36, :] = part[36:]
            between()

    def project_back(k):
        r0 = CHUNKS[k][0]
        across = wide[...].T.astype(BF)
        total = jnp.zeros((TOK, D), F32)
        for j in range(2):
            w = G[4 * j:4 * j + 4, :, r0:r0 + QR, :].reshape(8 * QR, D)
            total += dot(across[:, 8 * QR * j:8 * QR * (j + 1)], w, NN)
        return total

    def exchange_start(src, dst, i):
        def step(n, carry):
            t = (seq + n) % PARTS
            copy(src.at[t], dst.at[seq], as_.at[i], ar.at[i], (dp, t))
            return carry

        lax.fori_loop(1, PARTS, step, 0)
        dst[seq] = src[seq]

    def exchange_done(dst, i):
        drain(dst.at[pl.ds(0, PARTS - 1)], ar.at[i])

    def reduce0(t):
        copy(B.at[t, :, 1 - c], R0.at[t], rs.at[t, 0], rr.at[t, 0], sibling)

    def reduce1(t):
        drain(R0.at[t], rr.at[t, 0])
        for i in range(8):
            E[t, i // 2, i % 2] = (B[t, i, c].astype(F32) + R0[t, i].astype(F32)).astype(BF)
        for d in range(1, 4):
            xd, yd = (x + d) % 4, (y + d) % 4
            rows = pl.ds(pl.multiple_of(QTR * xd, 16), QTR)
            copy(E.at[t, :, 0, rows], R1.at[t, 0, d - 1], rs.at[t, 1], rr.at[t, 1], at(xd, y, Z, c))
            rows = pl.ds(pl.multiple_of(QTR * yd, 16), QTR)
            copy(E.at[t, :, 1, rows], R1.at[t, 1, d - 1], rs.at[t, 1], rr.at[t, 1], at(x, yd, Z, c))

    def reduce2(t):
        drain(R1.at[t], rr.at[t, 1])
        for side, at_ in enumerate((x, y)):
            rows = pl.ds(pl.multiple_of(QTR * at_, 16), QTR)
            for i in range(4):
                total = E[t, i, side, rows, :].astype(F32)
                for d in range(3):
                    total += R1[t, side, d, i].astype(F32)
                FS[side, i, 2 * t:2 * t + 2] = total.astype(BF).reshape(2, SUB, 128)

    def reduce3():
        for d in range(1, 4):
            xd, yd = (x + d) % 4, (y + d) % 4
            copy(FS.at[0, :, yd], R2.at[0, d - 1], rs.at[0, 2], rr.at[0, 2], at(x, yd, Z, c))
            copy(FS.at[1, :, xd], R2.at[1, d - 1], rs.at[0, 2], rr.at[0, 2], at(xd, y, Z, c))

    away = (-3, -2, -1, 1, 2, 3, 4)

    def reduce4():
        drain(R2, rr.at[0, 2])
        for side, at_ in enumerate((y, x)):
            for i in range(4):
                total = FS[side, i, at_].astype(F32)
                for d in range(3):
                    total += R2[side, d, i].astype(F32)
                H[2 * i + side] = total.astype(BF)
        for i, d in enumerate(away):
            there = (Z + 16 + d) % 16
            copy(H.at[there % 8], R3.at[i], rs.at[0, 3], rr.at[0, 3], at(x, y, there, c))

    def reduce5():
        drain(R3, rr.at[0, 3])
        total = H[z].astype(F32)
        for i in range(7):
            total += R3[i].astype(F32)
        Q[0] = total.astype(BF)
        copy(Q.at[0], R4, rs.at[0, 4], rr.at[0, 4], at(x, y, (Z + 8) % 16, c))

    even = z % 2 == 0
    quarter, part_of = jnp.where(even, x, y), jnp.where(even, y, x)

    def reduce6():
        drain(R4, rr.at[0, 4])
        total = (Q[0].astype(F32) + R4[...].astype(F32)).astype(BF)
        Q[1] = total
        OUT[4 * quarter + part_of] = total

        def step(n, carry):
            copy(Q.at[1], OUT.at[4 * quarter + part_of], rs.at[0, 5], rr.at[0, 5], plane(n))
            return carry

        lax.fori_loop(1, 16, step, 0)

    def reduce7():
        drain(OUT.at[pl.ds(0, 15)], rr.at[0, 5])
        for t, out in enumerate((d_time, d_space)):
            for q in range(4):
                for i in range(2):
                    start = QTR * q + SUB * i
                    tmp[start:start + SUB, :] = OUT[4 * q + 2 * t + i].astype(F32)
            for i in range(5):
                n = min(128, WIDTH - 128 * i)
                out[:, 128 * i:128 * i + n] = tmp[OC * i:OC * (i + 1), :n]

    def reduce_sent():
        for t in range(2):
            drain(R0.at[t], rs.at[t, 0])
            drain(R1.at[t], rs.at[t, 1])
        drain(R2, rs.at[0, 2])
        drain(R3, rs.at[0, 3])
        drain(R4, rs.at[0, 4])
        drain(OUT.at[pl.ds(0, 15)], rs.at[0, 5])

    pump(1)
    for i in (2, 3, 4):
        loading[i].wait()
    both = jnp.concatenate([out_s[...].astype(F32), out_t[...].astype(F32)], 1)
    G[z, c, QR:QR + OR, :] = jnp.concatenate(
        [both, jnp.zeros((OR - OC, D), F32)], 0
    ).astype(BF)
    own_columns(2, qkv_t)
    mixed_s[WIDTH:, :] = jnp.zeros((mixed_s.shape[0] - WIDTH, TOK), F32)
    mixed_t[:WIDTH, :] = jnp.zeros((WIDTH, TOK), F32)
    mixed_t[D:, :] = jnp.zeros((mixed_t.shape[0] - D, TOK), F32)
    loading[1].wait()
    loading[5].wait()
    hidden = tokens[...].astype(F32)
    xn = (normalize(hidden)[0] * gains[0:1, :]).astype(BF)
    need(0)
    project(0, xn, packed_s)
    pump(1)
    attend(packed_s, probs_s, mixed_s, 0, None, lambda: pump(1))
    need(1)
    middle = tokens[...].astype(F32) + project_out(mixed_s)
    send1[...] = middle.reshape(PARTS, 8, D).astype(BF)
    exchange_start(send1, recv1, 0)
    pump(2)
    send3[...] = mixed_s[0:640, :].T.reshape(PARTS, 8, 640).astype(BF)
    exchange_start(send3, recv3, 2)

    project_out_back(cot[...].astype(F32).reshape(TOK, D), 512, 64)
    need(2)
    exchange_done(recv1, 0)
    middle_t = recv1[...].astype(F32).reshape(TOK, D)
    normed, inv_std = normalize(middle_t)
    project(2, (normed * gains[1:2, :]).astype(BF), packed_t)
    mask = lax.broadcasted_iota(jnp.int32, (TOK, TOK), 0) % 8 == (
        lax.broadcasted_iota(jnp.int32, (TOK, TOK), 1) % 8
    )
    attend(packed_t, probs_t, mixed_t, WIDTH, mask, lambda: None)
    outer(mixed_t, WIDTH, B.at[0])
    reduce0(0)
    attend_back(packed_t, probs_t, lambda: None)
    d_xn = project_back(2)
    middle_t = recv1[...].astype(F32).reshape(TOK, D)
    normed, inv_std = normalize(middle_t)
    gain_time = jnp.sum(d_xn * normed, 0, keepdims=True)
    d_middle = cot[...].astype(F32).reshape(TOK, D) + norm_backward(
        d_xn, normed, inv_std, gains[1:2, :]
    )
    send2[...] = d_middle.reshape(PARTS, 8, D).astype(BF)
    exchange_start(send2, recv2, 1)
    reduce1(0)
    flat[...] = send2[...].astype(F32).reshape(TOK, D).T
    exchange_done(recv3, 2)
    mixed_p[...] = recv3[...].astype(F32).reshape(TOK, 640).T
    outer(mixed_p, 0, B.at[1])
    reduce0(1)
    out_t_ = project_out(mixed_t)
    reduce1(1)
    result[...] = (recv1[...].astype(F32) + out_t_.reshape(PARTS, 8, D)).astype(BF)
    reduce2(0)

    reduce2(1)
    reduce3()
    exchange_done(recv2, 1)
    frame = recv2[...].astype(F32).reshape(TOK, D)
    project_out_back(frame, 0, 0)
    reduce4()
    attend_back(packed_s, probs_s, lambda: None)
    d_xn = project_back(0)
    reduce5()
    normed, inv_std = normalize(tokens[...].astype(F32))
    gain_space = jnp.sum(d_xn * normed, 0, keepdims=True)

    gsend[...] = jnp.zeros(gsend.shape, F32)
    for j in range(PARTS):
        gsend[j:j + 1, 0:OC] = gain_space[:, OC * j:OC * (j + 1)]
        gsend[j:j + 1, 128:128 + OC] = gain_time[:, OC * j:OC * (j + 1)]
    mine = y * 4 + x
    gplane[mine] = gsend[...].astype(BF)

    def to_plane(n, carry):
        copy(gplane.at[mine], gplane.at[mine], ps.at[0], pr.at[0], plane(n))
        return carry

    lax.fori_loop(1, 16, to_plane, 0)
    d_tokens[...] = (
        recv2[...].astype(F32).reshape(TOK, D)
        + norm_backward(d_xn, normed, inv_std, gains[0:1, :])
    ).astype(BF)
    reduce6()
    drain(gplane.at[pl.ds(0, 15)], pr.at[0])
    total = gplane[0].astype(F32)
    for i in range(1, 16):
        total += gplane[i].astype(F32)
    for j in range(PARTS):
        gcol[j] = total[j:j + 1]
    me = Z * 2 + c

    def to_column(n, carry):
        other, device = column(n)
        copy(gcol.at[other % 16], gall.at[me], ps.at[1], pr.at[1], device)
        return carry

    lax.fori_loop(1, 32, to_column, 0)
    gall[me] = gcol[me % 16]
    reduce7()
    drain(gall.at[pl.ds(0, 31)], pr.at[1])
    total = gall[0]
    for i in range(1, 32):
        total += gall[i]
    d_gain[0:1, :] = total[:, 0:OC]
    d_gain[1:2, :] = total[:, 128:128 + OC]

    for k in range(3):
        drain(shards(k, 7), gs.at[k])
        drain(shards(k, 8), gss.at[k])
    drain(send1.at[pl.ds(0, 15)], as_.at[0])
    drain(send2.at[pl.ds(0, 15)], as_.at[1])
    drain(send3.at[pl.ds(0, 15)], as_.at[2])
    reduce_sent()
    drain(gplane.at[pl.ds(0, 15)], ps.at[0])
    drain(gall.at[pl.ds(0, 31)], ps.at[1])


def local(tokens, norm_gains, qkv_space, out_space, qkv_time, out_time, cotangent):
    vmem, sem = pltpu.VMEM, pltpu.SemaphoreType.DMA
    in_vmem = pl.BlockSpec(memory_space=pltpu.VMEM)
    anywhere = pl.BlockSpec(memory_space=pl.ANY)
    result, d_tokens, d_space, d_time, d_gain = pl.pallas_call(
        kernel,
        out_shape=(
            vmem((16, 8, D), BF),
            vmem((TOK, D), BF),
            vmem((OC, WIDTH), F32),
            vmem((OC, WIDTH), F32),
            vmem((2, OC), F32),
        ),
        in_specs=[anywhere, in_vmem] + [anywhere] * 5,
        out_specs=(in_vmem,) * 5,
        scratch_shapes=[
            vmem((TOK, D), BF),
            vmem((QC, D), BF),
            vmem((OC, WIDTH), BF),
            vmem((QC, D), BF),
            vmem((OC, WIDTH), BF),
            vmem((16, 8, D), BF),
            vmem((8, 2, ROWS, D), BF),
            vmem((3 * WIDTH, TOK), F32),
            vmem((3 * WIDTH, TOK), F32),
            vmem((HEADS, TOK, TOK), F32),
            vmem((HEADS, TOK, TOK), F32),
            vmem((D + 64, TOK), F32),
            vmem((D + 64, TOK), F32),
            vmem((640, TOK), F32),
            vmem((PARTS * QR, TOK), F32),
            vmem((D, TOK), F32),
            vmem((PARTS * OR, TOK), F32),
            vmem((WIDTH, TOK), F32),
            vmem((PARTS, 8, D), BF),
            vmem((PARTS, 8, D), BF),
            vmem((PARTS, 8, D), BF),
            vmem((PARTS, 8, D), BF),
            vmem((PARTS, 8, 640), BF),
            vmem((PARTS, 8, 640), BF),
            vmem((2, 8, 2, BLK, 128), BF),
            vmem((2, 8, BLK, 128), BF),
            vmem((2, 4, 2, BLK, 128), BF),
            vmem((2, 2, 3, 4, QTR, 128), BF),
            vmem((2, 4, 4, SUB, 128), BF),
            vmem((2, 3, 4, SUB, 128), BF),
            vmem((8, SUB, 128), BF),
            vmem((7, SUB, 128), BF),
            vmem((2, SUB, 128), BF),
            vmem((SUB, 128), BF),
            vmem((16, SUB, 128), BF),
            vmem((BLK, 128), F32),
            vmem((16, 256), F32),
            vmem((16, 16, 256), BF),
            vmem((16, 1, 256), F32),
            vmem((32, 1, 256), F32),
            sem((6,)),
            sem((3, 2, 4)),
            sem((3, 4)),
            sem((3, 4)),
            sem((3, 5)),
            sem((3,)),
            sem((3,)),
            sem((3,)),
            sem((3,)),
            sem((2, 6)),
            sem((2, 6)),
            sem((2,)),
            sem((2,)),
        ],
        compiler_params=pltpu.CompilerParams(
            collective_id=0, has_side_effects=True, vmem_limit_bytes=56 * 1024 * 1024
        ),
        name="block_pair",
    )(
        tokens.reshape(TOK, D), norm_gains, qkv_space.T, out_space.T, qkv_time.T, out_time.T,
        cotangent.reshape(16, 8, D),
    )
    return (
        result.reshape(1, 16, 8, D),
        d_tokens.reshape(1, 1, TOK, D),
        d_space.T,
        d_time.T,
        d_gain,
    )


def solution(mesh):
    return jax.shard_map(
        local,
        mesh=mesh,
        in_specs=(
            P("dp", "seq", None, None),
            P(),
            P(None, "seq"),
            P(None, "seq"),
            P(None, "seq"),
            P(None, "seq"),
            P("dp", None, "seq", None),
        ),
        out_specs=(
            P("dp", None, "seq", None),
            P("dp", "seq", None, None),
            P(None, "seq"),
            P(None, "seq"),
            P(None, "seq"),
        ),
        check_vma=False,
    )
```

```python
import functools

import jax
import jax.numpy as jnp
from jax import lax
from jax.experimental import pallas as pl
from jax.experimental.pallas import tpu as pltpu
from jax.sharding import PartitionSpec as P

HEADS = 8
HD = 72
WIDTH = HEADS * HD
D = 1152
PARTS = 16
QC = 3 * WIDTH // PARTS
OC = D // PARTS
QR = 112
OR = 80
CHUNKS = ((0, QR), (QR, OR), (QR + OR, QR))
ROWS = 2 * QR + OR
TOK = 128
BLK = 384
QTR = 96
SUB = 48
EPS = 1e-06
BF = jnp.bfloat16
F32 = jnp.float32
MESH = pl.DeviceIdType.MESH
NT = (((1,), (1,)), ((), ()))
NN = (((1,), (0,)), ((), ()))
TN = (((0,), (0,)), ((), ()))

ORDER = (
    "b00", "b10", "b20", "z01", "z11", "z02", "z12", "p01", "z21", "z03", "p02", "q01",
    "z13", "p03", "z04", "q02", "z14", "z22", "p12", "q03", "p13", "p04", "p11", "p14",
    "z23", "q04", "p22", "q11", "q12", "q14", "p21", "q13", "z24", "q22", "p23", "p24",
    "q21", "q23", "q24",
)


def dot(left, right, dims):
    return lax.dot_general(left, right, dims, preferred_element_type=F32)


def rounded(value):
    return value.astype(BF).astype(F32)


def normalize(hidden):
    average = jnp.mean(hidden, -1, keepdims=True)
    centered = hidden - average
    inv_std = lax.rsqrt(jnp.mean(centered * centered, -1, keepdims=True) + EPS)
    return centered * inv_std, inv_std


def norm_backward(upstream, normed, inv_std, gain):
    scaled = upstream * gain
    return inv_std * (
        scaled
        - jnp.mean(scaled, -1, keepdims=True)
        - normed * jnp.mean(scaled * normed, -1, keepdims=True)
    )


def widened(column):
    return (column // QC) * QR + column % QC


def kernel(
    tokens_in, gains, qkv_s_in, out_s_in, qkv_t_in, out_t_in, cot_in,
    result, d_tokens, d_space, d_time, d_gain,
    tokens, qkv_s, out_s, qkv_t, out_t, cot,
    G, packed_s, packed_t, probs_s, probs_t, mixed_s, mixed_t, mixed_p, wide, flat, flat_x, d_mix,
    send1, recv1, send2, recv2, send3, recv3,
    B, R0, E, R1, FS, R2, H, R3, Q, R4, OUT, tmp,
    gsend, gplane, gcol, gall, normed_s, inv_std_s,
    loads, zr, xy1, xy2, sb, gs, gss, as_, ar, rs, rr, ps, pr,
):
    dp, seq = lax.axis_index("dp"), lax.axis_index("seq")
    x, y, z_hi = dp % 4, (dp // 4) % 4, dp // 16
    z, c = seq // 2, seq % 2
    Z = z_hi * 8 + z

    def at(x_, y_, Z_, c_):
        return ((Z_ // 8) * 16 + y_ * 4 + x_, (Z_ % 8) * 2 + c_)

    def copy(src, dst, ssem, rsem, device):
        pltpu.make_async_remote_copy(
            src_ref=src, dst_ref=dst, send_sem=ssem, recv_sem=rsem,
            device_id=device, device_id_type=MESH,
        ).start()

    def drain(ref, sem):
        pltpu.make_async_copy(ref, ref, sem).wait()

    def plane(n):
        other = (y * 4 + x + n) % 16
        return at(other % 4, other // 4, Z, c)

    def column(n):
        other = (Z * 2 + c + n) % 32
        return other, at(x, y, other // 2, other % 2)

    right, left = at(x, y, (Z + 1) % 16, c), at(x, y, (Z + 15) % 16, c)
    sibling = at(x, y, Z, 1 - c)
    xp, xm = at((x + 1) % 4, y, Z, c), at((x + 3) % 4, y, Z, c)
    yp, ym = at(x, (y + 1) % 4, Z, c), at(x, (y + 3) % 4, Z, c)
    x2, y2 = at((x + 2) % 4, y, Z, c), at(x, (y + 2) % 4, Z, c)

    barrier = pltpu.get_barrier_semaphore()

    def greet(device):
        pl.semaphore_signal(barrier, inc=1, device_id=device, device_id_type=MESH)

    def greet_column(n, carry):
        greet(column(n)[1])
        greet(column(32 - n)[1])
        return carry

    def greet_plane(n, carry):
        greet(plane(n))
        greet(plane(16 - n))
        return carry

    lax.fori_loop(1, 5, greet_column, 0)
    lax.fori_loop(1, 8, greet_plane, 0)
    greet(plane(8))
    lax.fori_loop(5, 16, greet_column, 0)
    greet(column(16)[1])

    arrays = (
        (qkv_s_in, qkv_s), (tokens_in, tokens), (out_s_in, out_s), (out_t_in, out_t),
        (qkv_t_in, qkv_t), (cot_in, cot),
    )
    loading = [
        pltpu.make_async_copy(src, dst, loads.at[i]) for i, (src, dst) in enumerate(arrays)
    ]
    for load in loading:
        load.start()

    def own_columns(k, ref):
        r0, n = CHUNKS[k]
        G[z, c, r0:r0 + n, :] = jnp.concatenate(
            [ref[...].astype(F32), jnp.zeros((QR - QC, D), F32)], 0
        ).astype(BF)

    loading[0].wait()
    own_columns(0, qkv_s)
    pl.semaphore_wait(barrier, 46)

    units = (x, 4 + y, 8)

    def tile(zs, k, u):
        r0, n = CHUNKS[k]
        return G.at[zs, c, pl.ds(r0, n), pl.ds(pl.multiple_of(u * 128, 128), 128)]

    def lanes(k, n):
        r0, rows = CHUNKS[k]
        return G.at[0, 0, pl.ds(r0, rows), pl.ds(0, 128 * n)]

    def shards(k, n):
        r0, rows = CHUNKS[k]
        return G.at[pl.ds(0, n), 0, pl.ds(r0, rows), :]

    def whole(zs, k):
        r0, rows = CHUNKS[k]
        return G.at[zs, c, pl.ds(r0, rows), :]

    def hand_on(zs, k, u, rsem, device):
        copy(tile(zs, k, u), tile(zs, k, u), gs.at[k], rsem, device)

    def to_sibling(zs, k, h):
        copy(whole(zs, k), whole(zs, k), gss.at[k], sb.at[k, h], sibling)

    def begin(k):
        for u in units:
            hand_on(z, k, u, zr.at[k, 0, 0], right)
            hand_on(z, k, u, zr.at[k, 1, 0], left)
        to_sibling(z, k, 0)

    def from_z(k, h):
        zl, zq = (z + 8 - h) % 8, (z + h) % 8
        if h < 4:
            drain(lanes(k, 3), zr.at[k, 0, h - 1])
            for u in units if h < 3 else (units[1:] if k % 2 else units[1:2]):
                hand_on(zl, k, u, zr.at[k, 0, h], right)
            drain(lanes(k, 3), zr.at[k, 1, h - 1])
            for u in units if h < 3 else (units[:1] if k % 2 else units[::2]):
                hand_on(zq, k, u, zr.at[k, 1, h], left)
        else:
            drain(lanes(k, 2 if k % 2 else 1), zr.at[k, 0, 3])
            drain(lanes(k, 1 if k % 2 else 2), zr.at[k, 1, 3])
        for zs in (zl, zq) if h < 4 else (zl,):
            hand_on(zs, k, x, xy1.at[k, h - 1], xp)
            hand_on(zs, k, x, xy1.at[k, h - 1], xm)
            hand_on(zs, k, 4 + y, xy1.at[k, h - 1], yp)
            hand_on(zs, k, 4 + y, xy1.at[k, h - 1], ym)
            if direct(k, h):
                hand_on(zs, k, x, xy1.at[k, h - 1], x2)
                hand_on(zs, k, 4 + y, xy1.at[k, h - 1], y2)

    def direct(k, h):
        return k == 0 and h == 4

    def from_plane(k, h):
        zl, zq = (z + 8 - h) % 8, (z + h) % 8
        if direct(k, h):
            drain(lanes(k, 6), xy1.at[k, h - 1])
            to_sibling(zl, k, h)
            return
        drain(lanes(k, 8 if h < 4 else 4), xy1.at[k, h - 1])
        hand_on(zl, k, (x + 3) % 4, xy2.at[k, h - 1], xp)
        if h < 4:
            hand_on(zl, k, 4 + (y + 3) % 4, xy2.at[k, h - 1], yp)
            hand_on(zq, k, (x + 1) % 4, xy2.at[k, h - 1], xm)
        hand_on(zq, k, 4 + (y + 1) % 4, xy2.at[k, h - 1], ym)

    def last_of_plane(k, h):
        if direct(k, h):
            return
        zl, zq = (z + 8 - h) % 8, (z + h) % 8
        drain(lanes(k, 4 if h < 4 else 2), xy2.at[k, h - 1])
        for zs in (zl, zq) if h < 4 else (zl,):
            to_sibling(zs, k, h)

    acts = dict(b=begin, z=from_z, p=from_plane, q=last_of_plane)
    events = []
    for word in ORDER:
        kind, k, h = word[0], int(word[1]), int(word[2])
        where = (k,) if kind == "b" else (k, h)
        events.append((k, functools.partial(acts[kind], *where)))

    def pump(n):
        for _ in range(min(n, len(events))):
            events.pop(0)[1]()

    def need(k):
        while any(event[0] == k for event in events):
            pump(1)
        for h in range(5):
            drain(shards(k, 2 if 0 < h < 4 else 1), sb.at[k, h])

    def project(k, xn, packed):
        r0 = CHUNKS[k][0]
        for j in range(8):
            part = rounded(dot(G[j, :, r0:r0 + QR, :].reshape(2 * QR, D), xn, NT))
            packed[2 * QC * j:2 * QC * j + QC, :] = part[:QC]
            packed[2 * QC * j + QC:2 * QC * (j + 1), :] = part[QR:QR + QC]

    def heads_of(packed, h):
        return tuple(
            packed[i * WIDTH + HD * h:i * WIDTH + HD * (h + 1), :].astype(BF) for i in range(3)
        )

    def attend(packed, probs, mixed, start, mask, between):
        for h in range(HEADS):
            q, k, v = heads_of(packed, h)
            logits = dot(k, q, TN) * HD ** (-0.5)
            if mask is not None:
                logits = jnp.where(mask, logits, -1e30)
            raised = jnp.exp(logits - jnp.max(logits, 0, keepdims=True))
            p = raised / jnp.sum(raised, 0, keepdims=True)
            probs[h] = p
            mixed[start + HD * h:start + HD * (h + 1), :] = rounded(dot(v, p.astype(BF), NN))
            between()

    def project_out(mixed):
        m = mixed[0:D, :].astype(BF)
        for j in range(8):
            part = dot(G[j, :, QR:QR + OR, :].reshape(2 * OR, D), m, NN)
            flat[2 * OC * j:2 * OC * j + OC, :] = part[:OC]
            flat[2 * OC * j + OC:2 * OC * (j + 1), :] = part[OR:OR + OC]
        return flat[...].T

    def project_out_back(upstream, first, start):
        flat[...] = upstream.T
        for j in range(PARTS):
            flat_x[OR * j:OR * j + OC, :] = flat[OC * j:OC * (j + 1), :]
            flat_x[OR * j + OC:OR * (j + 1), :] = jnp.zeros((OR - OC, TOK), F32)
        across = flat_x[...].T.astype(BF)
        total = jnp.zeros((TOK, 640), F32)
        for j in range(2):
            w = G[4 * j:4 * j + 4, :, QR:QR + OR, first:first + 640].reshape(8 * OR, 640)
            total += dot(across[:, 8 * OR * j:8 * OR * (j + 1)], w, NN)
        d_mix[...] = rounded(total.T[start:start + WIDTH])

    def outer(mixed, start, blocks):
        m = mixed[start:start + 640, :].astype(BF)
        tmp[360:BLK, :] = jnp.zeros((BLK - 360, 128), F32)
        for j in range(4):
            part = dot(flat[4 * OC * j:4 * OC * (j + 1), :].astype(BF), m, NT)
            for i in range(4):
                for t in range(5):
                    tmp[OC * t:OC * (t + 1), :] = part[OC * i:OC * (i + 1), 128 * t:128 * (t + 1)]
                blocks[2 * j + i // 2, i % 2] = tmp[...].astype(BF)

    def attend_back(packed, probs, between):
        for j in range(PARTS):
            wide[QR * j + QC:QR * (j + 1), :] = jnp.zeros((QR - QC, TOK), F32)
        for h in range(HEADS):
            q, k, v = heads_of(packed, h)
            dm = d_mix[HD * h:HD * (h + 1), :].astype(BF)
            p = probs[h]
            d_w = dot(v, dm, TN)
            d_v = dot(dm, p.astype(BF), NT)
            d_s = (p * (d_w - jnp.sum(d_w * p, 0, keepdims=True)) * HD ** (-0.5)).astype(BF)
            for i, part in enumerate((dot(k, d_s, NN), dot(q, d_s, NT), d_v)):
                col = i * WIDTH + HD * h
                if widened(col + 36) == widened(col) + 36:
                    wide[widened(col):widened(col) + HD, :] = part
                else:
                    wide[widened(col):widened(col) + 36, :] = part[:36]
                    wide[widened(col + 36):widened(col + 36) + 36, :] = part[36:]
            between()

    def project_back(k):
        r0 = CHUNKS[k][0]
        across = wide[...].T.astype(BF)
        total = jnp.zeros((TOK, D), F32)
        for j in range(2):
            w = G[4 * j:4 * j + 4, :, r0:r0 + QR, :].reshape(8 * QR, D)
            total += dot(across[:, 8 * QR * j:8 * QR * (j + 1)], w, NN)
        return total

    def exchange_start(src, dst, i):
        def step(n, carry):
            t = (seq + n) % PARTS
            copy(src.at[t], dst.at[seq], as_.at[i], ar.at[i], (dp, t))
            return carry

        lax.fori_loop(1, PARTS, step, 0)
        dst[seq] = src[seq]

    def exchange_done(dst, i):
        drain(dst.at[pl.ds(0, PARTS - 1)], ar.at[i])

    def reduce0(t):
        copy(B.at[t, :, 1 - c], R0.at[t], rs.at[t, 0], rr.at[t, 0], sibling)

    def reduce1(t):
        drain(R0.at[t], rr.at[t, 0])
        for i in range(8):
            E[t, i // 2, i % 2] = (B[t, i, c].astype(F32) + R0[t, i].astype(F32)).astype(BF)
        for d in range(1, 4):
            xd, yd = (x + d) % 4, (y + d) % 4
            rows = pl.ds(pl.multiple_of(QTR * xd, 16), QTR)
            copy(E.at[t, :, 0, rows], R1.at[t, 0, d - 1], rs.at[t, 1], rr.at[t, 1], at(xd, y, Z, c))
            rows = pl.ds(pl.multiple_of(QTR * yd, 16), QTR)
            copy(E.at[t, :, 1, rows], R1.at[t, 1, d - 1], rs.at[t, 1], rr.at[t, 1], at(x, yd, Z, c))

    def reduce2(t):
        drain(R1.at[t], rr.at[t, 1])
        for side, at_ in enumerate((x, y)):
            rows = pl.ds(pl.multiple_of(QTR * at_, 16), QTR)
            for i in range(4):
                total = E[t, i, side, rows, :].astype(F32)
                for d in range(3):
                    total += R1[t, side, d, i].astype(F32)
                FS[side, i, 2 * t:2 * t + 2] = total.astype(BF).reshape(2, SUB, 128)

    def reduce3():
        for d in range(1, 4):
            xd, yd = (x + d) % 4, (y + d) % 4
            copy(FS.at[0, :, yd], R2.at[0, d - 1], rs.at[0, 2], rr.at[0, 2], at(x, yd, Z, c))
            copy(FS.at[1, :, xd], R2.at[1, d - 1], rs.at[0, 2], rr.at[0, 2], at(xd, y, Z, c))

    away = (-3, -2, -1, 1, 2, 3, 4)

    def reduce4():
        drain(R2, rr.at[0, 2])
        for side, at_ in enumerate((y, x)):
            for i in range(4):
                total = FS[side, i, at_].astype(F32)
                for d in range(3):
                    total += R2[side, d, i].astype(F32)
                H[2 * i + side] = total.astype(BF)
        for i, d in enumerate(away):
            there = (Z + 16 + d) % 16
            copy(H.at[there % 8], R3.at[i], rs.at[0, 3], rr.at[0, 3], at(x, y, there, c))

    def reduce5():
        drain(R3, rr.at[0, 3])
        total = H[z].astype(F32)
        for i in range(7):
            total += R3[i].astype(F32)
        Q[0] = total.astype(BF)
        copy(Q.at[0], R4, rs.at[0, 4], rr.at[0, 4], at(x, y, (Z + 8) % 16, c))

    even = z % 2 == 0
    quarter, part_of = jnp.where(even, x, y), jnp.where(even, y, x)

    def reduce6():
        drain(R4, rr.at[0, 4])
        total = (Q[0].astype(F32) + R4[...].astype(F32)).astype(BF)
        Q[1] = total
        OUT[4 * quarter + part_of] = total

        def step(n, carry):
            copy(Q.at[1], OUT.at[4 * quarter + part_of], rs.at[0, 5], rr.at[0, 5], plane(n))
            return carry

        lax.fori_loop(1, 16, step, 0)

    def reduce7():
        drain(OUT.at[pl.ds(0, 15)], rr.at[0, 5])
        for t, out in enumerate((d_time, d_space)):
            for q in range(4):
                for i in range(2):
                    start = QTR * q + SUB * i
                    tmp[start:start + SUB, :] = OUT[4 * q + 2 * t + i].astype(F32)
            for i in range(5):
                n = min(128, WIDTH - 128 * i)
                out[:, 128 * i:128 * i + n] = tmp[OC * i:OC * (i + 1), :n]

    def reduce_sent():
        for t in range(2):
            drain(R0.at[t], rs.at[t, 0])
            drain(R1.at[t], rs.at[t, 1])
        drain(R2, rs.at[0, 2])
        drain(R3, rs.at[0, 3])
        drain(R4, rs.at[0, 4])
        drain(OUT.at[pl.ds(0, 15)], rs.at[0, 5])

    pump(1)
    for i in (2, 3, 4):
        loading[i].wait()
    both = jnp.concatenate([out_s[...].astype(F32), out_t[...].astype(F32)], 1)
    G[z, c, QR:QR + OR, :] = jnp.concatenate(
        [both, jnp.zeros((OR - OC, D), F32)], 0
    ).astype(BF)
    own_columns(2, qkv_t)
    mixed_s[WIDTH:, :] = jnp.zeros((mixed_s.shape[0] - WIDTH, TOK), F32)
    mixed_t[:WIDTH, :] = jnp.zeros((WIDTH, TOK), F32)
    mixed_t[D:, :] = jnp.zeros((mixed_t.shape[0] - D, TOK), F32)
    loading[1].wait()
    loading[5].wait()
    normed, inv_std = normalize(tokens[...].astype(F32))
    normed_s[...], inv_std_s[...] = normed, inv_std
    xn = (normed * gains[0:1, :]).astype(BF)
    need(0)
    project(0, xn, packed_s)
    pump(1)
    attend(packed_s, probs_s, mixed_s, 0, None, lambda: pump(1))
    need(1)
    middle = tokens[...].astype(F32) + project_out(mixed_s)
    send1[...] = middle.reshape(PARTS, 8, D).astype(BF)
    exchange_start(send1, recv1, 0)
    pump(2)
    send3[...] = mixed_s[0:640, :].T.reshape(PARTS, 8, 640).astype(BF)
    exchange_start(send3, recv3, 2)

    project_out_back(cot[...].astype(F32).reshape(TOK, D), 512, 64)
    need(2)
    exchange_done(recv1, 0)
    middle_t = recv1[...].astype(F32).reshape(TOK, D)
    normed, inv_std = normalize(middle_t)
    project(2, (normed * gains[1:2, :]).astype(BF), packed_t)
    mask = lax.broadcasted_iota(jnp.int32, (TOK, TOK), 0) % 8 == (
        lax.broadcasted_iota(jnp.int32, (TOK, TOK), 1) % 8
    )
    attend(packed_t, probs_t, mixed_t, WIDTH, mask, lambda: None)
    outer(mixed_t, WIDTH, B.at[0])
    reduce0(0)
    turns = [lambda: None] * 4 + [lambda: reduce1(0)] + [lambda: None] * 3
    attend_back(packed_t, probs_t, lambda: turns.pop(0)())
    d_xn = project_back(2)
    middle_t = recv1[...].astype(F32).reshape(TOK, D)
    normed, inv_std = normalize(middle_t)
    gain_time = jnp.sum(d_xn * normed, 0, keepdims=True)
    d_middle = cot[...].astype(F32).reshape(TOK, D) + norm_backward(
        d_xn, normed, inv_std, gains[1:2, :]
    )
    send2[...] = d_middle.reshape(PARTS, 8, D).astype(BF)
    exchange_start(send2, recv2, 1)
    flat[...] = send2[...].astype(F32).reshape(TOK, D).T
    exchange_done(recv3, 2)
    mixed_p[...] = recv3[...].astype(F32).reshape(TOK, 640).T
    outer(mixed_p, 0, B.at[1])
    reduce0(1)
    reduce2(0)
    reduce1(1)
    out_t_ = project_out(mixed_t)
    result[...] = (recv1[...].astype(F32) + out_t_.reshape(PARTS, 8, D)).astype(BF)

    reduce2(1)
    reduce3()
    exchange_done(recv2, 1)
    frame = recv2[...].astype(F32).reshape(TOK, D)
    project_out_back(frame, 0, 0)
    reduce4()
    attend_back(packed_s, probs_s, lambda: None)
    d_xn = project_back(0)
    gain_space = jnp.sum(d_xn * normed_s[...], 0, keepdims=True)

    gsend[...] = jnp.zeros(gsend.shape, F32)
    for j in range(PARTS):
        gsend[j:j + 1, 0:OC] = gain_space[:, OC * j:OC * (j + 1)]
        gsend[j:j + 1, 128:128 + OC] = gain_time[:, OC * j:OC * (j + 1)]
    mine = y * 4 + x
    gplane[mine] = gsend[...].astype(BF)

    def to_plane(n, carry):
        copy(gplane.at[mine], gplane.at[mine], ps.at[0], pr.at[0], plane(n))
        return carry

    lax.fori_loop(1, 16, to_plane, 0)
    reduce5()
    d_tokens[...] = (
        recv2[...].astype(F32).reshape(TOK, D)
        + norm_backward(d_xn, normed_s[...], inv_std_s[...], gains[0:1, :])
    ).astype(BF)
    drain(gplane.at[pl.ds(0, 15)], pr.at[0])
    total = gplane[0].astype(F32)
    for i in range(1, 16):
        total += gplane[i].astype(F32)
    for j in range(PARTS):
        gcol[j] = total[j:j + 1]
    me = Z * 2 + c

    def to_column(n, carry):
        other, device = column(n)
        copy(gcol.at[other % 16], gall.at[me], ps.at[1], pr.at[1], device)
        return carry

    lax.fori_loop(1, 32, to_column, 0)
    gall[me] = gcol[me % 16]
    reduce6()
    drain(gall.at[pl.ds(0, 31)], pr.at[1])
    total = gall[0]
    for i in range(1, 32):
        total += gall[i]
    d_gain[0:1, :] = total[:, 0:OC]
    d_gain[1:2, :] = total[:, 128:128 + OC]
    reduce7()

    for k in range(3):
        drain(shards(k, 7), gs.at[k])
        drain(shards(k, 8), gss.at[k])
    drain(send1.at[pl.ds(0, 15)], as_.at[0])
    drain(send2.at[pl.ds(0, 15)], as_.at[1])
    drain(send3.at[pl.ds(0, 15)], as_.at[2])
    reduce_sent()
    drain(gplane.at[pl.ds(0, 15)], ps.at[0])
    drain(gall.at[pl.ds(0, 31)], ps.at[1])


def local(tokens, norm_gains, qkv_space, out_space, qkv_time, out_time, cotangent):
    vmem, sem = pltpu.VMEM, pltpu.SemaphoreType.DMA
    in_vmem = pl.BlockSpec(memory_space=pltpu.VMEM)
    anywhere = pl.BlockSpec(memory_space=pl.ANY)
    result, d_tokens, d_space, d_time, d_gain = pl.pallas_call(
        kernel,
        out_shape=(
            vmem((16, 8, D), BF),
            vmem((TOK, D), BF),
            vmem((OC, WIDTH), F32),
            vmem((OC, WIDTH), F32),
            vmem((2, OC), F32),
        ),
        in_specs=[anywhere, in_vmem] + [anywhere] * 5,
        out_specs=(in_vmem,) * 5,
        scratch_shapes=[
            vmem((TOK, D), BF),
            vmem((QC, D), BF),
            vmem((OC, WIDTH), BF),
            vmem((QC, D), BF),
            vmem((OC, WIDTH), BF),
            vmem((16, 8, D), BF),
            vmem((8, 2, ROWS, D), BF),
            vmem((3 * WIDTH, TOK), F32),
            vmem((3 * WIDTH, TOK), F32),
            vmem((HEADS, TOK, TOK), F32),
            vmem((HEADS, TOK, TOK), F32),
            vmem((D + 64, TOK), F32),
            vmem((D + 64, TOK), F32),
            vmem((640, TOK), F32),
            vmem((PARTS * QR, TOK), F32),
            vmem((D, TOK), F32),
            vmem((PARTS * OR, TOK), F32),
            vmem((WIDTH, TOK), F32),
            vmem((PARTS, 8, D), BF),
            vmem((PARTS, 8, D), BF),
            vmem((PARTS, 8, D), BF),
            vmem((PARTS, 8, D), BF),
            vmem((PARTS, 8, 640), BF),
            vmem((PARTS, 8, 640), BF),
            vmem((2, 8, 2, BLK, 128), BF),
            vmem((2, 8, BLK, 128), BF),
            vmem((2, 4, 2, BLK, 128), BF),
            vmem((2, 2, 3, 4, QTR, 128), BF),
            vmem((2, 4, 4, SUB, 128), BF),
            vmem((2, 3, 4, SUB, 128), BF),
            vmem((8, SUB, 128), BF),
            vmem((7, SUB, 128), BF),
            vmem((2, SUB, 128), BF),
            vmem((SUB, 128), BF),
            vmem((16, SUB, 128), BF),
            vmem((BLK, 128), F32),
            vmem((16, 256), F32),
            vmem((16, 16, 256), BF),
            vmem((16, 1, 256), F32),
            vmem((32, 1, 256), F32),
            vmem((TOK, D), F32),
            vmem((TOK, 1), F32),
            sem((6,)),
            sem((3, 2, 4)),
            sem((3, 4)),
            sem((3, 4)),
            sem((3, 5)),
            sem((3,)),
            sem((3,)),
            sem((3,)),
            sem((3,)),
            sem((2, 6)),
            sem((2, 6)),
            sem((2,)),
            sem((2,)),
        ],
        compiler_params=pltpu.CompilerParams(
            collective_id=0, has_side_effects=True, vmem_limit_bytes=56 * 1024 * 1024
        ),
        name="block_pair",
    )(
        tokens.reshape(TOK, D), norm_gains, qkv_space.T, out_space.T, qkv_time.T, out_time.T,
        cotangent.reshape(16, 8, D),
    )
    return (
        result.reshape(1, 16, 8, D),
        d_tokens.reshape(1, 1, TOK, D),
        d_space.T,
        d_time.T,
        d_gain,
    )


def solution(mesh):
    return jax.shard_map(
        local,
        mesh=mesh,
        in_specs=(
            P("dp", "seq", None, None),
            P(),
            P(None, "seq"),
            P(None, "seq"),
            P(None, "seq"),
            P(None, "seq"),
            P("dp", None, "seq", None),
        ),
        out_specs=(
            P("dp", None, "seq", None),
            P("dp", "seq", None, None),
            P(None, "seq"),
            P(None, "seq"),
            P(None, "seq"),
        ),
        check_vma=False,
    )
```

```python
import functools

import jax
import jax.numpy as jnp
from jax import lax
from jax.experimental import pallas as pl
from jax.experimental.pallas import tpu as pltpu
from jax.sharding import PartitionSpec as P

HEADS = 8
HD = 72
WIDTH = HEADS * HD
D = 1152
PARTS = 16
QC = 3 * WIDTH // PARTS
OC = D // PARTS
QR = 112
OR = 80
CHUNKS = ((0, 64), (64, 48), (112, 80), (192, 64), (256, 48))
SPACE, OUTS, TIME = 0, QR, QR + OR
ROWS = 2 * QR + OR
TOK = 128
BLK = 384
QTR = 96
SUB = 48
EPS = 1e-06
BF = jnp.bfloat16
F32 = jnp.float32
MESH = pl.DeviceIdType.MESH
NT = (((1,), (1,)), ((), ()))
NN = (((1,), (0,)), ((), ()))
TN = (((0,), (0,)), ((), ()))

ORDER = (
    "b10", "b00", "b20", "z11", "z01", "z21", "z12", "p11", "z02", "p01", "b40", "z22",
    "z13", "p12", "q11", "z03", "p02", "b30", "z41", "p22", "p13", "z23", "q12", "p03",
    "z04", "z14", "z31", "q22", "q13", "z24", "q01", "q03", "p23", "p21", "q02", "p41",
    "p04", "z42", "p14", "q04", "z32", "p24", "q14", "q21", "q23", "z43", "z33", "q24",
    "p31", "q41", "p42", "p32", "z44", "z34", "p33", "q31", "q42", "p43", "p34", "p44",
    "q33", "q32", "q34", "q44", "q43",
)


def dot(left, right, dims):
    return lax.dot_general(left, right, dims, preferred_element_type=F32)


def rounded(value):
    return value.astype(BF).astype(F32)


def normalize(hidden):
    average = jnp.mean(hidden, -1, keepdims=True)
    centered = hidden - average
    inv_std = lax.rsqrt(jnp.mean(centered * centered, -1, keepdims=True) + EPS)
    return centered * inv_std, inv_std


def norm_backward(upstream, normed, inv_std, gain):
    scaled = upstream * gain
    return inv_std * (
        scaled
        - jnp.mean(scaled, -1, keepdims=True)
        - normed * jnp.mean(scaled * normed, -1, keepdims=True)
    )


def widened(column):
    return (column // QC) * QR + column % QC


def kernel(
    tokens_in, gains, qkv_s_in, out_s_in, qkv_t_in, out_t_in, cot_in,
    result, d_tokens, d_space, d_time, d_gain,
    tokens, qkv_s, out_s, qkv_t, out_t, cot,
    G, packed_s, packed_t, probs_s, probs_t, mixed_s, mixed_t, mixed_p, wide, flat, flat_x, d_mix,
    send1, recv1, send2, recv2, send3, recv3,
    B, R0, E, R1, FS, R2, H, R3, Q, R4, OUT, tmp,
    gsend, gplane, gcol, gall, normed_s, inv_std_s,
    loads, zr, xy1, xy2, sb, gs, gss, as_, ar, rs, rr, ps, pr,
):
    dp, seq = lax.axis_index("dp"), lax.axis_index("seq")
    x, y, z_hi = dp % 4, (dp // 4) % 4, dp // 16
    z, c = seq // 2, seq % 2
    Z = z_hi * 8 + z

    def at(x_, y_, Z_, c_):
        return ((Z_ // 8) * 16 + y_ * 4 + x_, (Z_ % 8) * 2 + c_)

    def copy(src, dst, ssem, rsem, device):
        pltpu.make_async_remote_copy(
            src_ref=src, dst_ref=dst, send_sem=ssem, recv_sem=rsem,
            device_id=device, device_id_type=MESH,
        ).start()

    def drain(ref, sem):
        pltpu.make_async_copy(ref, ref, sem).wait()

    def plane(n):
        other = (y * 4 + x + n) % 16
        return at(other % 4, other // 4, Z, c)

    def column(n):
        other = (Z * 2 + c + n) % 32
        return other, at(x, y, other // 2, other % 2)

    right, left = at(x, y, (Z + 1) % 16, c), at(x, y, (Z + 15) % 16, c)
    sibling = at(x, y, Z, 1 - c)
    xp, xm = at((x + 1) % 4, y, Z, c), at((x + 3) % 4, y, Z, c)
    yp, ym = at(x, (y + 1) % 4, Z, c), at(x, (y + 3) % 4, Z, c)
    x2, y2 = at((x + 2) % 4, y, Z, c), at(x, (y + 2) % 4, Z, c)

    barrier = pltpu.get_barrier_semaphore()

    near = (sibling, right, left, xp, xm, yp, ym)
    for device in near:
        pl.semaphore_signal(barrier, inc=1, device_id=device, device_id_type=MESH)

    arrays = (
        (qkv_s_in, qkv_s), (tokens_in, tokens), (out_s_in, out_s), (out_t_in, out_t),
        (qkv_t_in, qkv_t), (cot_in, cot),
    )
    loading = [
        pltpu.make_async_copy(src, dst, loads.at[i]) for i, (src, dst) in enumerate(arrays)
    ]
    for load in loading:
        load.start()

    def own_columns(r0, ref):
        G[z, c, r0:r0 + QR, :] = jnp.concatenate(
            [ref[...].astype(F32), jnp.zeros((QR - QC, D), F32)], 0
        ).astype(BF)

    loading[0].wait()
    own_columns(SPACE, qkv_s)
    pl.semaphore_wait(barrier, len(near))

    units = (x, 4 + y, 8)

    def tile(zs, k, u):
        r0, n = CHUNKS[k]
        return G.at[zs, c, pl.ds(r0, n), pl.ds(pl.multiple_of(u * 128, 128), 128)]

    def lanes(k, n):
        r0, rows = CHUNKS[k]
        return G.at[0, 0, pl.ds(r0, rows), pl.ds(0, 128 * n)]

    def shards(k, n):
        r0, rows = CHUNKS[k]
        return G.at[pl.ds(0, n), 0, pl.ds(r0, rows), :]

    def whole(zs, k):
        r0, rows = CHUNKS[k]
        return G.at[zs, c, pl.ds(r0, rows), :]

    def hand_on(zs, k, u, rsem, device):
        copy(tile(zs, k, u), tile(zs, k, u), gs.at[k], rsem, device)

    def to_sibling(zs, k, h):
        copy(whole(zs, k), whole(zs, k), gss.at[k], sb.at[k, h], sibling)

    def begin(k):
        for u in units:
            hand_on(z, k, u, zr.at[k, 0, 0], right)
            hand_on(z, k, u, zr.at[k, 1, 0], left)
        to_sibling(z, k, 0)

    def from_z(k, h):
        zl, zq = (z + 8 - h) % 8, (z + h) % 8
        if h < 4:
            drain(lanes(k, 3), zr.at[k, 0, h - 1])
            for u in units if h < 3 else (units[1:] if k % 2 else units[1:2]):
                hand_on(zl, k, u, zr.at[k, 0, h], right)
            drain(lanes(k, 3), zr.at[k, 1, h - 1])
            for u in units if h < 3 else (units[:1] if k % 2 else units[::2]):
                hand_on(zq, k, u, zr.at[k, 1, h], left)
        else:
            drain(lanes(k, 2 if k % 2 else 1), zr.at[k, 0, 3])
            drain(lanes(k, 1 if k % 2 else 2), zr.at[k, 1, 3])
        for zs in (zl, zq) if h < 4 else (zl,):
            hand_on(zs, k, x, xy1.at[k, h - 1], xp)
            hand_on(zs, k, x, xy1.at[k, h - 1], xm)
            hand_on(zs, k, 4 + y, xy1.at[k, h - 1], yp)
            hand_on(zs, k, 4 + y, xy1.at[k, h - 1], ym)
            if direct(k, h):
                hand_on(zs, k, x, xy1.at[k, h - 1], x2)
                hand_on(zs, k, 4 + y, xy1.at[k, h - 1], y2)

    def direct(k, h):
        return k < 2 and h == 4

    def from_plane(k, h):
        zl, zq = (z + 8 - h) % 8, (z + h) % 8
        if direct(k, h):
            drain(lanes(k, 6), xy1.at[k, h - 1])
            to_sibling(zl, k, h)
            return
        drain(lanes(k, 8 if h < 4 else 4), xy1.at[k, h - 1])
        hand_on(zl, k, (x + 3) % 4, xy2.at[k, h - 1], xp)
        if h < 4:
            hand_on(zl, k, 4 + (y + 3) % 4, xy2.at[k, h - 1], yp)
            hand_on(zq, k, (x + 1) % 4, xy2.at[k, h - 1], xm)
        hand_on(zq, k, 4 + (y + 1) % 4, xy2.at[k, h - 1], ym)

    def last_of_plane(k, h):
        if direct(k, h):
            return
        zl, zq = (z + 8 - h) % 8, (z + h) % 8
        drain(lanes(k, 4 if h < 4 else 2), xy2.at[k, h - 1])
        for zs in (zl, zq) if h < 4 else (zl,):
            to_sibling(zs, k, h)

    acts = dict(b=begin, z=from_z, p=from_plane, q=last_of_plane)
    events = []
    for word in ORDER:
        kind, k, h = word[0], int(word[1]), int(word[2])
        where = (k,) if kind == "b" else (k, h)
        events.append((k, functools.partial(acts[kind], *where)))

    def pump(n):
        for _ in range(min(n, len(events))):
            events.pop(0)[1]()

    def need(*chunks):
        while any(event[0] in chunks for event in events):
            pump(1)
        for k in chunks:
            for h in range(5):
                drain(shards(k, 2 if 0 < h < 4 else 1), sb.at[k, h])

    def project(r0, xn, packed):
        for j in range(8):
            part = rounded(dot(G[j, :, r0:r0 + QR, :].reshape(2 * QR, D), xn, NT))
            packed[2 * QC * j:2 * QC * j + QC, :] = part[:QC]
            packed[2 * QC * j + QC:2 * QC * (j + 1), :] = part[QR:QR + QC]

    def heads_of(packed, h):
        return tuple(
            packed[i * WIDTH + HD * h:i * WIDTH + HD * (h + 1), :].astype(BF) for i in range(3)
        )

    def attend(packed, probs, mixed, start, mask, between):
        for h in range(HEADS):
            q, k, v = heads_of(packed, h)
            logits = dot(k, q, TN) * HD ** (-0.5)
            if mask is not None:
                logits = jnp.where(mask, logits, -1e30)
            raised = jnp.exp(logits - jnp.max(logits, 0, keepdims=True))
            p = raised / jnp.sum(raised, 0, keepdims=True)
            probs[h] = p
            mixed[start + HD * h:start + HD * (h + 1), :] = rounded(dot(v, p.astype(BF), NN))
            between()

    def project_out(mixed):
        m = mixed[0:D, :].astype(BF)
        for j in range(8):
            part = dot(G[j, :, QR:QR + OR, :].reshape(2 * OR, D), m, NN)
            flat[2 * OC * j:2 * OC * j + OC, :] = part[:OC]
            flat[2 * OC * j + OC:2 * OC * (j + 1), :] = part[OR:OR + OC]
        return flat[...].T

    def project_out_back(upstream, first, start):
        flat[...] = upstream.T
        for j in range(PARTS):
            flat_x[OR * j:OR * j + OC, :] = flat[OC * j:OC * (j + 1), :]
            flat_x[OR * j + OC:OR * (j + 1), :] = jnp.zeros((OR - OC, TOK), F32)
        across = flat_x[...].T.astype(BF)
        total = jnp.zeros((TOK, 640), F32)
        for j in range(2):
            w = G[4 * j:4 * j + 4, :, QR:QR + OR, first:first + 640].reshape(8 * OR, 640)
            total += dot(across[:, 8 * OR * j:8 * OR * (j + 1)], w, NN)
        d_mix[...] = rounded(total.T[start:start + WIDTH])

    def outer(mixed, start, blocks):
        m = mixed[start:start + 640, :].astype(BF)
        tmp[360:BLK, :] = jnp.zeros((BLK - 360, 128), F32)
        for j in range(4):
            part = dot(flat[4 * OC * j:4 * OC * (j + 1), :].astype(BF), m, NT)
            for i in range(4):
                for t in range(5):
                    tmp[OC * t:OC * (t + 1), :] = part[OC * i:OC * (i + 1), 128 * t:128 * (t + 1)]
                blocks[2 * j + i // 2, i % 2] = tmp[...].astype(BF)

    def attend_back(packed, probs, between):
        for j in range(PARTS):
            wide[QR * j + QC:QR * (j + 1), :] = jnp.zeros((QR - QC, TOK), F32)
        for h in range(HEADS):
            q, k, v = heads_of(packed, h)
            dm = d_mix[HD * h:HD * (h + 1), :].astype(BF)
            p = probs[h]
            d_w = dot(v, dm, TN)
            d_v = dot(dm, p.astype(BF), NT)
            d_s = (p * (d_w - jnp.sum(d_w * p, 0, keepdims=True)) * HD ** (-0.5)).astype(BF)
            for i, part in enumerate((dot(k, d_s, NN), dot(q, d_s, NT), d_v)):
                col = i * WIDTH + HD * h
                if widened(col + 36) == widened(col) + 36:
                    wide[widened(col):widened(col) + HD, :] = part
                else:
                    wide[widened(col):widened(col) + 36, :] = part[:36]
                    wide[widened(col + 36):widened(col + 36) + 36, :] = part[36:]
            between()

    def project_back(r0):
        across = wide[...].T.astype(BF)
        total = jnp.zeros((TOK, D), F32)
        for j in range(2):
            w = G[4 * j:4 * j + 4, :, r0:r0 + QR, :].reshape(8 * QR, D)
            total += dot(across[:, 8 * QR * j:8 * QR * (j + 1)], w, NN)
        return total

    def exchange_start(src, dst, i):
        def step(n, carry):
            t = (seq + n) % PARTS
            copy(src.at[t], dst.at[seq], as_.at[i], ar.at[i], (dp, t))
            return carry

        lax.fori_loop(1, PARTS, step, 0)
        dst[seq] = src[seq]

    def exchange_done(dst, i):
        drain(dst.at[pl.ds(0, PARTS - 1)], ar.at[i])

    def reduce0(t):
        copy(B.at[t, :, 1 - c], R0.at[t], rs.at[t, 0], rr.at[t, 0], sibling)

    def reduce1(t):
        drain(R0.at[t], rr.at[t, 0])
        for i in range(8):
            E[t, i // 2, i % 2] = (B[t, i, c].astype(F32) + R0[t, i].astype(F32)).astype(BF)
        for d in range(1, 4):
            xd, yd = (x + d) % 4, (y + d) % 4
            rows = pl.ds(pl.multiple_of(QTR * xd, 16), QTR)
            copy(E.at[t, :, 0, rows], R1.at[t, 0, d - 1], rs.at[t, 1], rr.at[t, 1], at(xd, y, Z, c))
            rows = pl.ds(pl.multiple_of(QTR * yd, 16), QTR)
            copy(E.at[t, :, 1, rows], R1.at[t, 1, d - 1], rs.at[t, 1], rr.at[t, 1], at(x, yd, Z, c))

    def reduce2(t):
        drain(R1.at[t], rr.at[t, 1])
        for side, at_ in enumerate((x, y)):
            rows = pl.ds(pl.multiple_of(QTR * at_, 16), QTR)
            for i in range(4):
                total = E[t, i, side, rows, :].astype(F32)
                for d in range(3):
                    total += R1[t, side, d, i].astype(F32)
                FS[side, i, 2 * t:2 * t + 2] = total.astype(BF).reshape(2, SUB, 128)

    def reduce3():
        for d in range(1, 4):
            xd, yd = (x + d) % 4, (y + d) % 4
            copy(FS.at[0, :, yd], R2.at[0, d - 1], rs.at[0, 2], rr.at[0, 2], at(x, yd, Z, c))
            copy(FS.at[1, :, xd], R2.at[1, d - 1], rs.at[0, 2], rr.at[0, 2], at(xd, y, Z, c))

    away = (-3, -2, -1, 1, 2, 3, 4)

    def reduce4():
        drain(R2, rr.at[0, 2])
        for side, at_ in enumerate((y, x)):
            for i in range(4):
                total = FS[side, i, at_].astype(F32)
                for d in range(3):
                    total += R2[side, d, i].astype(F32)
                H[2 * i + side] = total.astype(BF)
        for i, d in enumerate(away):
            there = (Z + 16 + d) % 16
            copy(H.at[there % 8], R3.at[i], rs.at[0, 3], rr.at[0, 3], at(x, y, there, c))

    def reduce5():
        drain(R3, rr.at[0, 3])
        total = H[z].astype(F32)
        for i in range(7):
            total += R3[i].astype(F32)
        Q[0] = total.astype(BF)
        copy(Q.at[0], R4, rs.at[0, 4], rr.at[0, 4], at(x, y, (Z + 8) % 16, c))

    even = z % 2 == 0
    quarter, part_of = jnp.where(even, x, y), jnp.where(even, y, x)

    def reduce6():
        drain(R4, rr.at[0, 4])
        total = (Q[0].astype(F32) + R4[...].astype(F32)).astype(BF)
        Q[1] = total
        OUT[4 * quarter + part_of] = total

        def step(n, carry):
            copy(Q.at[1], OUT.at[4 * quarter + part_of], rs.at[0, 5], rr.at[0, 5], plane(n))
            return carry

        lax.fori_loop(1, 16, step, 0)

    def reduce7():
        drain(OUT.at[pl.ds(0, 15)], rr.at[0, 5])
        for t, out in enumerate((d_time, d_space)):
            for q in range(4):
                for i in range(2):
                    start = QTR * q + SUB * i
                    tmp[start:start + SUB, :] = OUT[4 * q + 2 * t + i].astype(F32)
            for i in range(5):
                n = min(128, WIDTH - 128 * i)
                out[:, 128 * i:128 * i + n] = tmp[OC * i:OC * (i + 1), :n]

    def reduce_sent():
        for t in range(2):
            drain(R0.at[t], rs.at[t, 0])
            drain(R1.at[t], rs.at[t, 1])
        drain(R2, rs.at[0, 2])
        drain(R3, rs.at[0, 3])
        drain(R4, rs.at[0, 4])
        drain(OUT.at[pl.ds(0, 15)], rs.at[0, 5])

    pump(2)
    for i in (2, 3, 4):
        loading[i].wait()
    both = jnp.concatenate([out_s[...].astype(F32), out_t[...].astype(F32)], 1)
    G[z, c, QR:QR + OR, :] = jnp.concatenate(
        [both, jnp.zeros((OR - OC, D), F32)], 0
    ).astype(BF)
    own_columns(TIME, qkv_t)
    mixed_s[WIDTH:, :] = jnp.zeros((mixed_s.shape[0] - WIDTH, TOK), F32)
    mixed_t[:WIDTH, :] = jnp.zeros((WIDTH, TOK), F32)
    mixed_t[D:, :] = jnp.zeros((mixed_t.shape[0] - D, TOK), F32)
    loading[1].wait()
    loading[5].wait()
    normed, inv_std = normalize(tokens[...].astype(F32))
    normed_s[...], inv_std_s[...] = normed, inv_std
    xn = (normed * gains[0:1, :]).astype(BF)
    need(0, 1)
    project(SPACE, xn, packed_s)
    pump(1)
    attend(packed_s, probs_s, mixed_s, 0, None, lambda: pump(1))
    need(2)
    middle = tokens[...].astype(F32) + project_out(mixed_s)
    send1[...] = middle.reshape(PARTS, 8, D).astype(BF)
    exchange_start(send1, recv1, 0)
    pump(2)
    send3[...] = mixed_s[0:640, :].T.reshape(PARTS, 8, 640).astype(BF)
    exchange_start(send3, recv3, 2)

    project_out_back(cot[...].astype(F32).reshape(TOK, D), 512, 64)
    need(3, 4)
    exchange_done(recv1, 0)
    middle_t = recv1[...].astype(F32).reshape(TOK, D)
    normed, inv_std = normalize(middle_t)
    project(TIME, (normed * gains[1:2, :]).astype(BF), packed_t)
    mask = lax.broadcasted_iota(jnp.int32, (TOK, TOK), 0) % 8 == (
        lax.broadcasted_iota(jnp.int32, (TOK, TOK), 1) % 8
    )
    attend(packed_t, probs_t, mixed_t, WIDTH, mask, lambda: None)
    outer(mixed_t, WIDTH, B.at[0])
    reduce0(0)
    turns = [lambda: None] * 4 + [lambda: reduce1(0)] + [lambda: None] * 3
    attend_back(packed_t, probs_t, lambda: turns.pop(0)())
    d_xn = project_back(TIME)
    middle_t = recv1[...].astype(F32).reshape(TOK, D)
    normed, inv_std = normalize(middle_t)
    gain_time = jnp.sum(d_xn * normed, 0, keepdims=True)
    d_middle = cot[...].astype(F32).reshape(TOK, D) + norm_backward(
        d_xn, normed, inv_std, gains[1:2, :]
    )
    send2[...] = d_middle.reshape(PARTS, 8, D).astype(BF)
    flat[...] = rounded(d_middle).T
    exchange_done(recv3, 2)
    mixed_p[...] = recv3[...].astype(F32).reshape(TOK, 640).T
    outer(mixed_p, 0, B.at[1])
    reduce0(1)
    exchange_start(send2, recv2, 1)
    reduce1(1)
    reduce2(0)
    out_t_ = project_out(mixed_t)
    result[...] = (recv1[...].astype(F32) + out_t_.reshape(PARTS, 8, D)).astype(BF)

    reduce2(1)
    reduce3()
    exchange_done(recv2, 1)
    frame = recv2[...].astype(F32).reshape(TOK, D)
    project_out_back(frame, 0, 0)
    attend_back(packed_s, probs_s, lambda: None)
    reduce4()
    d_xn = project_back(SPACE)
    gain_space = jnp.sum(d_xn * normed_s[...], 0, keepdims=True)

    gsend[...] = jnp.zeros(gsend.shape, F32)
    for j in range(PARTS):
        gsend[j:j + 1, 0:OC] = gain_space[:, OC * j:OC * (j + 1)]
        gsend[j:j + 1, 128:128 + OC] = gain_time[:, OC * j:OC * (j + 1)]
    mine = y * 4 + x
    gplane[mine] = gsend[...].astype(BF)

    def to_plane(n, carry):
        copy(gplane.at[mine], gplane.at[mine], ps.at[0], pr.at[0], plane(n))
        return carry

    lax.fori_loop(1, 16, to_plane, 0)
    d_tokens[...] = (
        recv2[...].astype(F32).reshape(TOK, D)
        + norm_backward(d_xn, normed_s[...], inv_std_s[...], gains[0:1, :])
    ).astype(BF)
    reduce5()
    drain(gplane.at[pl.ds(0, 15)], pr.at[0])
    total = gplane[0].astype(F32)
    for i in range(1, 16):
        total += gplane[i].astype(F32)
    for j in range(PARTS):
        gcol[j] = total[j:j + 1]
    me = Z * 2 + c

    def to_column(n, carry):
        other, device = column(n)
        copy(gcol.at[other % 16], gall.at[me], ps.at[1], pr.at[1], device)
        return carry

    lax.fori_loop(1, 32, to_column, 0)
    gall[me] = gcol[me % 16]
    reduce6()
    drain(gall.at[pl.ds(0, 31)], pr.at[1])
    total = gall[0]
    for i in range(1, 32):
        total += gall[i]
    d_gain[0:1, :] = total[:, 0:OC]
    d_gain[1:2, :] = total[:, 128:128 + OC]
    reduce7()

    for k in range(len(CHUNKS)):
        drain(shards(k, 7), gs.at[k])
        drain(shards(k, 8), gss.at[k])
    drain(send1.at[pl.ds(0, 15)], as_.at[0])
    drain(send2.at[pl.ds(0, 15)], as_.at[1])
    drain(send3.at[pl.ds(0, 15)], as_.at[2])
    reduce_sent()
    drain(gplane.at[pl.ds(0, 15)], ps.at[0])
    drain(gall.at[pl.ds(0, 31)], ps.at[1])


def local(tokens, norm_gains, qkv_space, out_space, qkv_time, out_time, cotangent):
    vmem, sem = pltpu.VMEM, pltpu.SemaphoreType.DMA
    in_vmem = pl.BlockSpec(memory_space=pltpu.VMEM)
    anywhere = pl.BlockSpec(memory_space=pl.ANY)
    result, d_tokens, d_space, d_time, d_gain = pl.pallas_call(
        kernel,
        out_shape=(
            vmem((16, 8, D), BF),
            vmem((TOK, D), BF),
            vmem((OC, WIDTH), F32),
            vmem((OC, WIDTH), F32),
            vmem((2, OC), F32),
        ),
        in_specs=[anywhere, in_vmem] + [anywhere] * 5,
        out_specs=(in_vmem,) * 5,
        scratch_shapes=[
            vmem((TOK, D), BF),
            vmem((QC, D), BF),
            vmem((OC, WIDTH), BF),
            vmem((QC, D), BF),
            vmem((OC, WIDTH), BF),
            vmem((16, 8, D), BF),
            vmem((8, 2, ROWS, D), BF),
            vmem((3 * WIDTH, TOK), F32),
            vmem((3 * WIDTH, TOK), F32),
            vmem((HEADS, TOK, TOK), F32),
            vmem((HEADS, TOK, TOK), F32),
            vmem((D + 64, TOK), F32),
            vmem((D + 64, TOK), F32),
            vmem((640, TOK), F32),
            vmem((PARTS * QR, TOK), F32),
            vmem((D, TOK), F32),
            vmem((PARTS * OR, TOK), F32),
            vmem((WIDTH, TOK), F32),
            vmem((PARTS, 8, D), BF),
            vmem((PARTS, 8, D), BF),
            vmem((PARTS, 8, D), BF),
            vmem((PARTS, 8, D), BF),
            vmem((PARTS, 8, 640), BF),
            vmem((PARTS, 8, 640), BF),
            vmem((2, 8, 2, BLK, 128), BF),
            vmem((2, 8, BLK, 128), BF),
            vmem((2, 4, 2, BLK, 128), BF),
            vmem((2, 2, 3, 4, QTR, 128), BF),
            vmem((2, 4, 4, SUB, 128), BF),
            vmem((2, 3, 4, SUB, 128), BF),
            vmem((8, SUB, 128), BF),
            vmem((7, SUB, 128), BF),
            vmem((2, SUB, 128), BF),
            vmem((SUB, 128), BF),
            vmem((16, SUB, 128), BF),
            vmem((BLK, 128), F32),
            vmem((16, 256), F32),
            vmem((16, 16, 256), BF),
            vmem((16, 1, 256), F32),
            vmem((32, 1, 256), F32),
            vmem((TOK, D), F32),
            vmem((TOK, 1), F32),
            sem((6,)),
            sem((5, 2, 4)),
            sem((5, 4)),
            sem((5, 4)),
            sem((5, 5)),
            sem((5,)),
            sem((5,)),
            sem((3,)),
            sem((3,)),
            sem((2, 6)),
            sem((2, 6)),
            sem((2,)),
            sem((2,)),
        ],
        compiler_params=pltpu.CompilerParams(
            collective_id=0, has_side_effects=True, vmem_limit_bytes=56 * 1024 * 1024
        ),
        name="block_pair",
    )(
        tokens.reshape(TOK, D), norm_gains, qkv_space.T, out_space.T, qkv_time.T, out_time.T,
        cotangent.reshape(16, 8, D),
    )
    return (
        result.reshape(1, 16, 8, D),
        d_tokens.reshape(1, 1, TOK, D),
        d_space.T,
        d_time.T,
        d_gain,
    )


def solution(mesh):
    return jax.shard_map(
        local,
        mesh=mesh,
        in_specs=(
            P("dp", "seq", None, None),
            P(),
            P(None, "seq"),
            P(None, "seq"),
            P(None, "seq"),
            P(None, "seq"),
            P("dp", None, "seq", None),
        ),
        out_specs=(
            P("dp", None, "seq", None),
            P("dp", "seq", None, None),
            P(None, "seq"),
            P(None, "seq"),
            P(None, "seq"),
        ),
        check_vma=False,
    )
```

```python
import functools

import jax
import jax.numpy as jnp
from jax import lax
from jax.experimental import pallas as pl
from jax.experimental.pallas import tpu as pltpu
from jax.sharding import PartitionSpec as P

HEADS = 8
HD = 72
WIDTH = HEADS * HD
D = 1152
PARTS = 16
QC = 3 * WIDTH // PARTS
OC = D // PARTS
QR = 112
OR = 80
CHUNKS = ((0, 64), (64, 48), (112, 80), (192, 64), (256, 48))
SPACE, OUTS, TIME = 0, QR, QR + OR
ROWS = 2 * QR + OR
TOK = 128
BLK = 384
QTR = 96
SUB = 48
EPS = 1e-06
BF = jnp.bfloat16
F32 = jnp.float32
MESH = pl.DeviceIdType.MESH
NT = (((1,), (1,)), ((), ()))
NN = (((1,), (0,)), ((), ()))
TN = (((0,), (0,)), ((), ()))

ORDER = (
    "b10", "b00", "b20", "z11", "z01", "z21", "z12", "p11", "z02", "p01", "b40", "z22",
    "z13", "p12", "q11", "z03", "p02", "b30", "z41", "p22", "p13", "z23", "q12", "p03",
    "z04", "z14", "z31", "q22", "q13", "z24", "q01", "q03", "p23", "p21", "q02", "p41",
    "p04", "z42", "p14", "q04", "z32", "p24", "q14", "q21", "q23", "z43", "z33", "q24",
    "p31", "q41", "p42", "p32", "z44", "z34", "p33", "q31", "q42", "p43", "p34", "p44",
    "q33", "q32", "q34", "q44", "q43",
)


def dot(left, right, dims):
    return lax.dot_general(left, right, dims, preferred_element_type=F32)


def rounded(value):
    return value.astype(BF).astype(F32)


def normalize(hidden):
    average = jnp.mean(hidden, -1, keepdims=True)
    centered = hidden - average
    inv_std = lax.rsqrt(jnp.mean(centered * centered, -1, keepdims=True) + EPS)
    return centered * inv_std, inv_std


def norm_backward(upstream, normed, inv_std, gain):
    scaled = upstream * gain
    return inv_std * (
        scaled
        - jnp.mean(scaled, -1, keepdims=True)
        - normed * jnp.mean(scaled * normed, -1, keepdims=True)
    )


def widened(column):
    return (column // QC) * QR + column % QC


def kernel(
    tokens_in, gains, qkv_s_in, out_s_in, qkv_t_in, out_t_in, cot_in,
    result, d_tokens, d_space, d_time, d_gain,
    tokens, qkv_s, out_s, qkv_t, out_t, cot,
    G, packed_s, packed_t, probs_s, probs_t, mixed_s, mixed_t, mixed_p, wide, flat, flat_x, d_mix,
    send1, recv1, send2, recv2, send3, recv3,
    B, R0, E, R1, FS, R2, H, R3, Q, R4, OUT, tmp,
    gsend, gplane, gcol, gall, normed_s, inv_std_s,
    loads, zr, xy1, xy2, sb, gs, gss, as_, ar, rs, rr, ps, pr,
):
    dp, seq = lax.axis_index("dp"), lax.axis_index("seq")
    x, y, z_hi = dp % 4, (dp // 4) % 4, dp // 16
    z, c = seq // 2, seq % 2
    Z = z_hi * 8 + z

    def at(x_, y_, Z_, c_):
        return ((Z_ // 8) * 16 + y_ * 4 + x_, (Z_ % 8) * 2 + c_)

    def copy(src, dst, ssem, rsem, device):
        pltpu.make_async_remote_copy(
            src_ref=src, dst_ref=dst, send_sem=ssem, recv_sem=rsem,
            device_id=device, device_id_type=MESH,
        ).start()

    def drain(ref, sem):
        pltpu.make_async_copy(ref, ref, sem).wait()

    def plane(n):
        other = (y * 4 + x + n) % 16
        return at(other % 4, other // 4, Z, c)

    def column(n):
        other = (Z * 2 + c + n) % 32
        return other, at(x, y, other // 2, other % 2)

    right, left = at(x, y, (Z + 1) % 16, c), at(x, y, (Z + 15) % 16, c)
    sibling = at(x, y, Z, 1 - c)
    xp, xm = at((x + 1) % 4, y, Z, c), at((x + 3) % 4, y, Z, c)
    yp, ym = at(x, (y + 1) % 4, Z, c), at(x, (y + 3) % 4, Z, c)
    x2, y2 = at((x + 2) % 4, y, Z, c), at(x, (y + 2) % 4, Z, c)

    barrier = pltpu.get_barrier_semaphore()

    near = (sibling, right, left, xp, xm, yp, ym)
    for device in near:
        pl.semaphore_signal(barrier, inc=1, device_id=device, device_id_type=MESH)

    arrays = (
        (qkv_s_in, qkv_s), (tokens_in, tokens), (out_s_in, out_s), (out_t_in, out_t),
        (qkv_t_in, qkv_t), (cot_in, cot),
    )
    loading = [
        pltpu.make_async_copy(src, dst, loads.at[i]) for i, (src, dst) in enumerate(arrays)
    ]
    for load in loading:
        load.start()

    def own_columns(r0, ref):
        G[z, c, r0:r0 + QR, :] = jnp.concatenate(
            [ref[...].astype(F32), jnp.zeros((QR - QC, D), F32)], 0
        ).astype(BF)

    loading[0].wait()
    own_columns(SPACE, qkv_s)
    pl.semaphore_wait(barrier, len(near))

    units = (x, 4 + y, 8)

    def tile(zs, k, u):
        r0, n = CHUNKS[k]
        return G.at[zs, c, pl.ds(r0, n), pl.ds(pl.multiple_of(u * 128, 128), 128)]

    def lanes(k, n):
        r0, rows = CHUNKS[k]
        return G.at[0, 0, pl.ds(r0, rows), pl.ds(0, 128 * n)]

    def shards(k, n):
        r0, rows = CHUNKS[k]
        return G.at[pl.ds(0, n), 0, pl.ds(r0, rows), :]

    def whole(zs, k):
        r0, rows = CHUNKS[k]
        return G.at[zs, c, pl.ds(r0, rows), :]

    def hand_on(zs, k, u, rsem, device):
        copy(tile(zs, k, u), tile(zs, k, u), gs.at[k], rsem, device)

    def to_sibling(zs, k, h):
        copy(whole(zs, k), whole(zs, k), gss.at[k], sb.at[k, h], sibling)

    def begin(k):
        for u in units:
            hand_on(z, k, u, zr.at[k, 0, 0], right)
            hand_on(z, k, u, zr.at[k, 1, 0], left)
        to_sibling(z, k, 0)

    def from_z(k, h):
        zl, zq = (z + 8 - h) % 8, (z + h) % 8
        if h < 4:
            drain(lanes(k, 3), zr.at[k, 0, h - 1])
            for u in units if h < 3 else (units[1:] if k % 2 else units[1:2]):
                hand_on(zl, k, u, zr.at[k, 0, h], right)
            drain(lanes(k, 3), zr.at[k, 1, h - 1])
            for u in units if h < 3 else (units[:1] if k % 2 else units[::2]):
                hand_on(zq, k, u, zr.at[k, 1, h], left)
        else:
            drain(lanes(k, 2 if k % 2 else 1), zr.at[k, 0, 3])
            drain(lanes(k, 1 if k % 2 else 2), zr.at[k, 1, 3])
        for zs in (zl, zq) if h < 4 else (zl,):
            hand_on(zs, k, x, xy1.at[k, h - 1], xp)
            hand_on(zs, k, x, xy1.at[k, h - 1], xm)
            hand_on(zs, k, 4 + y, xy1.at[k, h - 1], yp)
            hand_on(zs, k, 4 + y, xy1.at[k, h - 1], ym)
            if direct(k, h):
                hand_on(zs, k, x, xy1.at[k, h - 1], x2)
                hand_on(zs, k, 4 + y, xy1.at[k, h - 1], y2)

    def direct(k, h):
        return k < 2 and h == 4

    def from_plane(k, h):
        zl, zq = (z + 8 - h) % 8, (z + h) % 8
        if direct(k, h):
            drain(lanes(k, 6), xy1.at[k, h - 1])
            to_sibling(zl, k, h)
            return
        drain(lanes(k, 8 if h < 4 else 4), xy1.at[k, h - 1])
        hand_on(zl, k, (x + 3) % 4, xy2.at[k, h - 1], xp)
        if h < 4:
            hand_on(zl, k, 4 + (y + 3) % 4, xy2.at[k, h - 1], yp)
            hand_on(zq, k, (x + 1) % 4, xy2.at[k, h - 1], xm)
        hand_on(zq, k, 4 + (y + 1) % 4, xy2.at[k, h - 1], ym)

    def last_of_plane(k, h):
        if direct(k, h):
            return
        zl, zq = (z + 8 - h) % 8, (z + h) % 8
        drain(lanes(k, 4 if h < 4 else 2), xy2.at[k, h - 1])
        for zs in (zl, zq) if h < 4 else (zl,):
            to_sibling(zs, k, h)

    acts = dict(b=begin, z=from_z, p=from_plane, q=last_of_plane)
    events = []
    for word in ORDER:
        kind, k, h = word[0], int(word[1]), int(word[2])
        where = (k,) if kind == "b" else (k, h)
        events.append((k, functools.partial(acts[kind], *where)))

    def pump(n):
        for _ in range(min(n, len(events))):
            events.pop(0)[1]()

    def need(*chunks):
        while any(event[0] in chunks for event in events):
            pump(1)
        for k in chunks:
            for h in range(5):
                drain(shards(k, 2 if 0 < h < 4 else 1), sb.at[k, h])

    def project(r0, xn, packed):
        for j in range(8):
            part = rounded(dot(G[j, :, r0:r0 + QR, :].reshape(2 * QR, D), xn, NT))
            packed[2 * QC * j:2 * QC * j + QC, :] = part[:QC]
            packed[2 * QC * j + QC:2 * QC * (j + 1), :] = part[QR:QR + QC]

    def heads_of(packed, h):
        return tuple(
            packed[i * WIDTH + HD * h:i * WIDTH + HD * (h + 1), :].astype(BF) for i in range(3)
        )

    def attend(packed, probs, mixed, start, mask, between):
        for h in range(HEADS):
            q, k, v = heads_of(packed, h)
            logits = dot(k, q, TN) * HD ** (-0.5)
            if mask is not None:
                logits = jnp.where(mask, logits, -1e30)
            raised = jnp.exp(logits - jnp.max(logits, 0, keepdims=True))
            p = raised / jnp.sum(raised, 0, keepdims=True)
            probs[h] = p
            mixed[start + HD * h:start + HD * (h + 1), :] = rounded(dot(v, p.astype(BF), NN))
            between()

    def project_out(mixed):
        m = mixed[0:D, :].astype(BF)
        for j in range(8):
            part = dot(G[j, :, QR:QR + OR, :].reshape(2 * OR, D), m, NN)
            flat[2 * OC * j:2 * OC * j + OC, :] = part[:OC]
            flat[2 * OC * j + OC:2 * OC * (j + 1), :] = part[OR:OR + OC]
        return flat[...].T

    def project_out_back(upstream, first, start):
        flat[...] = upstream.T
        for j in range(PARTS):
            flat_x[OR * j:OR * j + OC, :] = flat[OC * j:OC * (j + 1), :]
            flat_x[OR * j + OC:OR * (j + 1), :] = jnp.zeros((OR - OC, TOK), F32)
        across = flat_x[...].T.astype(BF)
        total = jnp.zeros((TOK, 640), F32)
        for j in range(2):
            w = G[4 * j:4 * j + 4, :, QR:QR + OR, first:first + 640].reshape(8 * OR, 640)
            total += dot(across[:, 8 * OR * j:8 * OR * (j + 1)], w, NN)
        d_mix[...] = rounded(total.T[start:start + WIDTH])

    def outer(mixed, start, blocks):
        m = mixed[start:start + 640, :].astype(BF)
        tmp[360:BLK, :] = jnp.zeros((BLK - 360, 128), F32)
        for j in range(4):
            part = dot(flat[4 * OC * j:4 * OC * (j + 1), :].astype(BF), m, NT)
            for i in range(4):
                for t in range(5):
                    tmp[OC * t:OC * (t + 1), :] = part[OC * i:OC * (i + 1), 128 * t:128 * (t + 1)]
                blocks[2 * j + i // 2, i % 2] = tmp[...].astype(BF)

    def attend_back(packed, probs, between):
        for j in range(PARTS):
            wide[QR * j + QC:QR * (j + 1), :] = jnp.zeros((QR - QC, TOK), F32)
        for h in range(HEADS):
            q, k, v = heads_of(packed, h)
            dm = d_mix[HD * h:HD * (h + 1), :].astype(BF)
            p = probs[h]
            d_w = dot(v, dm, TN)
            d_v = dot(dm, p.astype(BF), NT)
            d_s = (p * (d_w - jnp.sum(d_w * p, 0, keepdims=True)) * HD ** (-0.5)).astype(BF)
            for i, part in enumerate((dot(k, d_s, NN), dot(q, d_s, NT), d_v)):
                col = i * WIDTH + HD * h
                if widened(col + 36) == widened(col) + 36:
                    wide[widened(col):widened(col) + HD, :] = part
                else:
                    wide[widened(col):widened(col) + 36, :] = part[:36]
                    wide[widened(col + 36):widened(col + 36) + 36, :] = part[36:]
            between()

    def project_back(r0):
        across = wide[...].T.astype(BF)
        total = jnp.zeros((TOK, D), F32)
        for j in range(2):
            w = G[4 * j:4 * j + 4, :, r0:r0 + QR, :].reshape(8 * QR, D)
            total += dot(across[:, 8 * QR * j:8 * QR * (j + 1)], w, NN)
        return total

    def exchange_start(src, dst, i):
        for n in (8, 9, 7, 10, 6, 11, 5, 12, 4, 13, 3, 14, 2, 15, 1):
            t = (seq + n) % PARTS
            copy(src.at[t], dst.at[seq], as_.at[i], ar.at[i], (dp, t))
        dst[seq] = src[seq]

    def exchange_done(dst, i):
        drain(dst.at[pl.ds(0, PARTS - 1)], ar.at[i])

    def reduce0(t):
        copy(B.at[t, :, 1 - c], R0.at[t], rs.at[t, 0], rr.at[t, 0], sibling)

    def reduce1(t):
        drain(R0.at[t], rr.at[t, 0])
        for i in range(8):
            E[t, i // 2, i % 2] = (B[t, i, c].astype(F32) + R0[t, i].astype(F32)).astype(BF)
        for d in range(1, 4):
            xd, yd = (x + d) % 4, (y + d) % 4
            rows = pl.ds(pl.multiple_of(QTR * xd, 16), QTR)
            copy(E.at[t, :, 0, rows], R1.at[t, 0, d - 1], rs.at[t, 1], rr.at[t, 1], at(xd, y, Z, c))
            rows = pl.ds(pl.multiple_of(QTR * yd, 16), QTR)
            copy(E.at[t, :, 1, rows], R1.at[t, 1, d - 1], rs.at[t, 1], rr.at[t, 1], at(x, yd, Z, c))

    def reduce2(t):
        drain(R1.at[t], rr.at[t, 1])
        for side, at_ in enumerate((x, y)):
            rows = pl.ds(pl.multiple_of(QTR * at_, 16), QTR)
            for i in range(4):
                total = E[t, i, side, rows, :].astype(F32)
                for d in range(3):
                    total += R1[t, side, d, i].astype(F32)
                FS[side, i, 2 * t:2 * t + 2] = total.astype(BF).reshape(2, SUB, 128)

    def reduce3():
        for d in range(1, 4):
            xd, yd = (x + d) % 4, (y + d) % 4
            copy(FS.at[0, :, yd], R2.at[0, d - 1], rs.at[0, 2], rr.at[0, 2], at(x, yd, Z, c))
            copy(FS.at[1, :, xd], R2.at[1, d - 1], rs.at[0, 2], rr.at[0, 2], at(xd, y, Z, c))

    away = (-3, -2, -1, 1, 2, 3, 4)

    def reduce4():
        drain(R2, rr.at[0, 2])
        for side, at_ in enumerate((y, x)):
            for i in range(4):
                total = FS[side, i, at_].astype(F32)
                for d in range(3):
                    total += R2[side, d, i].astype(F32)
                H[2 * i + side] = total.astype(BF)
        for i, d in enumerate(away):
            there = (Z + 16 + d) % 16
            copy(H.at[there % 8], R3.at[i], rs.at[0, 3], rr.at[0, 3], at(x, y, there, c))

    def reduce5():
        drain(R3, rr.at[0, 3])
        total = H[z].astype(F32)
        for i in range(7):
            total += R3[i].astype(F32)
        Q[0] = total.astype(BF)
        copy(Q.at[0], R4, rs.at[0, 4], rr.at[0, 4], at(x, y, (Z + 8) % 16, c))

    even = z % 2 == 0
    quarter, part_of = jnp.where(even, x, y), jnp.where(even, y, x)

    def reduce6():
        drain(R4, rr.at[0, 4])
        total = (Q[0].astype(F32) + R4[...].astype(F32)).astype(BF)
        Q[1] = total
        OUT[4 * quarter + part_of] = total

        def step(n, carry):
            copy(Q.at[1], OUT.at[4 * quarter + part_of], rs.at[0, 5], rr.at[0, 5], plane(n))
            return carry

        lax.fori_loop(1, 16, step, 0)

    def reduce7():
        drain(OUT.at[pl.ds(0, 15)], rr.at[0, 5])
        for t, out in enumerate((d_time, d_space)):
            for q in range(4):
                for i in range(2):
                    start = QTR * q + SUB * i
                    tmp[start:start + SUB, :] = OUT[4 * q + 2 * t + i].astype(F32)
            for i in range(5):
                n = min(128, WIDTH - 128 * i)
                out[:, 128 * i:128 * i + n] = tmp[OC * i:OC * (i + 1), :n]

    def reduce_sent():
        for t in range(2):
            drain(R0.at[t], rs.at[t, 0])
            drain(R1.at[t], rs.at[t, 1])
        drain(R2, rs.at[0, 2])
        drain(R3, rs.at[0, 3])
        drain(R4, rs.at[0, 4])
        drain(OUT.at[pl.ds(0, 15)], rs.at[0, 5])

    pump(2)
    for i in (2, 3, 4):
        loading[i].wait()
    both = jnp.concatenate([out_s[...].astype(F32), out_t[...].astype(F32)], 1)
    G[z, c, QR:QR + OR, :] = jnp.concatenate(
        [both, jnp.zeros((OR - OC, D), F32)], 0
    ).astype(BF)
    own_columns(TIME, qkv_t)
    mixed_s[WIDTH:, :] = jnp.zeros((mixed_s.shape[0] - WIDTH, TOK), F32)
    mixed_t[:WIDTH, :] = jnp.zeros((WIDTH, TOK), F32)
    mixed_t[D:, :] = jnp.zeros((mixed_t.shape[0] - D, TOK), F32)
    loading[1].wait()
    loading[5].wait()
    normed, inv_std = normalize(tokens[...].astype(F32))
    normed_s[...], inv_std_s[...] = normed, inv_std
    xn = (normed * gains[0:1, :]).astype(BF)
    need(0, 1)
    project(SPACE, xn, packed_s)
    pump(1)
    attend(packed_s, probs_s, mixed_s, 0, None, lambda: pump(1))
    need(2)
    middle = tokens[...].astype(F32) + project_out(mixed_s)
    send1[...] = middle.reshape(PARTS, 8, D).astype(BF)
    exchange_start(send1, recv1, 0)
    pump(2)
    send3[...] = mixed_s[0:640, :].T.reshape(PARTS, 8, 640).astype(BF)
    exchange_start(send3, recv3, 2)

    project_out_back(cot[...].astype(F32).reshape(TOK, D), 512, 64)
    need(3, 4)
    exchange_done(recv1, 0)
    middle_t = recv1[...].astype(F32).reshape(TOK, D)
    normed, inv_std = normalize(middle_t)
    project(TIME, (normed * gains[1:2, :]).astype(BF), packed_t)
    mask = lax.broadcasted_iota(jnp.int32, (TOK, TOK), 0) % 8 == (
        lax.broadcasted_iota(jnp.int32, (TOK, TOK), 1) % 8
    )
    attend(packed_t, probs_t, mixed_t, WIDTH, mask, lambda: None)
    outer(mixed_t, WIDTH, B.at[0])
    reduce0(0)
    turns = [lambda: None] * 4 + [lambda: reduce1(0)] + [lambda: None] * 3
    attend_back(packed_t, probs_t, lambda: turns.pop(0)())
    d_xn = project_back(TIME)
    middle_t = recv1[...].astype(F32).reshape(TOK, D)
    normed, inv_std = normalize(middle_t)
    gain_time = jnp.sum(d_xn * normed, 0, keepdims=True)
    d_middle = cot[...].astype(F32).reshape(TOK, D) + norm_backward(
        d_xn, normed, inv_std, gains[1:2, :]
    )
    send2[...] = d_middle.reshape(PARTS, 8, D).astype(BF)
    flat[...] = rounded(d_middle).T
    exchange_done(recv3, 2)
    mixed_p[...] = recv3[...].astype(F32).reshape(TOK, 640).T
    outer(mixed_p, 0, B.at[1])
    reduce0(1)
    exchange_start(send2, recv2, 1)
    reduce1(1)
    reduce2(0)
    out_t_ = project_out(mixed_t)
    result[...] = (recv1[...].astype(F32) + out_t_.reshape(PARTS, 8, D)).astype(BF)

    reduce2(1)
    reduce3()
    exchange_done(recv2, 1)
    frame = recv2[...].astype(F32).reshape(TOK, D)
    project_out_back(frame, 0, 0)
    attend_back(packed_s, probs_s, lambda: None)
    reduce4()
    d_xn = project_back(SPACE)
    gain_space = jnp.sum(d_xn * normed_s[...], 0, keepdims=True)

    gsend[...] = jnp.zeros(gsend.shape, F32)
    for j in range(PARTS):
        gsend[j:j + 1, 0:OC] = gain_space[:, OC * j:OC * (j + 1)]
        gsend[j:j + 1, 128:128 + OC] = gain_time[:, OC * j:OC * (j + 1)]
    mine = y * 4 + x
    gplane[mine] = gsend[...].astype(BF)

    def to_plane(n, carry):
        copy(gplane.at[mine], gplane.at[mine], ps.at[0], pr.at[0], plane(n))
        return carry

    lax.fori_loop(1, 16, to_plane, 0)
    d_tokens[...] = (
        recv2[...].astype(F32).reshape(TOK, D)
        + norm_backward(d_xn, normed_s[...], inv_std_s[...], gains[0:1, :])
    ).astype(BF)
    reduce5()
    drain(gplane.at[pl.ds(0, 15)], pr.at[0])
    total = gplane[0].astype(F32)
    for i in range(1, 16):
        total += gplane[i].astype(F32)
    for j in range(PARTS):
        gcol[j] = total[j:j + 1]
    me = Z * 2 + c

    def to_column(n, carry):
        other, device = column(n)
        copy(gcol.at[other % 16], gall.at[me], ps.at[1], pr.at[1], device)
        return carry

    lax.fori_loop(1, 32, to_column, 0)
    gall[me] = gcol[me % 16]
    reduce6()
    drain(gall.at[pl.ds(0, 31)], pr.at[1])
    total = gall[0]
    for i in range(1, 32):
        total += gall[i]
    d_gain[0:1, :] = total[:, 0:OC]
    d_gain[1:2, :] = total[:, 128:128 + OC]
    reduce7()

    for k in range(len(CHUNKS)):
        drain(shards(k, 7), gs.at[k])
        drain(shards(k, 8), gss.at[k])
    drain(send1.at[pl.ds(0, 15)], as_.at[0])
    drain(send2.at[pl.ds(0, 15)], as_.at[1])
    drain(send3.at[pl.ds(0, 15)], as_.at[2])
    reduce_sent()
    drain(gplane.at[pl.ds(0, 15)], ps.at[0])
    drain(gall.at[pl.ds(0, 31)], ps.at[1])


def local(tokens, norm_gains, qkv_space, out_space, qkv_time, out_time, cotangent):
    vmem, sem = pltpu.VMEM, pltpu.SemaphoreType.DMA
    in_vmem = pl.BlockSpec(memory_space=pltpu.VMEM)
    anywhere = pl.BlockSpec(memory_space=pl.ANY)
    result, d_tokens, d_space, d_time, d_gain = pl.pallas_call(
        kernel,
        out_shape=(
            vmem((16, 8, D), BF),
            vmem((TOK, D), BF),
            vmem((OC, WIDTH), F32),
            vmem((OC, WIDTH), F32),
            vmem((2, OC), F32),
        ),
        in_specs=[anywhere, in_vmem] + [anywhere] * 5,
        out_specs=(in_vmem,) * 5,
        scratch_shapes=[
            vmem((TOK, D), BF),
            vmem((QC, D), BF),
            vmem((OC, WIDTH), BF),
            vmem((QC, D), BF),
            vmem((OC, WIDTH), BF),
            vmem((16, 8, D), BF),
            vmem((8, 2, ROWS, D), BF),
            vmem((3 * WIDTH, TOK), F32),
            vmem((3 * WIDTH, TOK), F32),
            vmem((HEADS, TOK, TOK), F32),
            vmem((HEADS, TOK, TOK), F32),
            vmem((D + 64, TOK), F32),
            vmem((D + 64, TOK), F32),
            vmem((640, TOK), F32),
            vmem((PARTS * QR, TOK), F32),
            vmem((D, TOK), F32),
            vmem((PARTS * OR, TOK), F32),
            vmem((WIDTH, TOK), F32),
            vmem((PARTS, 8, D), BF),
            vmem((PARTS, 8, D), BF),
            vmem((PARTS, 8, D), BF),
            vmem((PARTS, 8, D), BF),
            vmem((PARTS, 8, 640), BF),
            vmem((PARTS, 8, 640), BF),
            vmem((2, 8, 2, BLK, 128), BF),
            vmem((2, 8, BLK, 128), BF),
            vmem((2, 4, 2, BLK, 128), BF),
            vmem((2, 2, 3, 4, QTR, 128), BF),
            vmem((2, 4, 4, SUB, 128), BF),
            vmem((2, 3, 4, SUB, 128), BF),
            vmem((8, SUB, 128), BF),
            vmem((7, SUB, 128), BF),
            vmem((2, SUB, 128), BF),
            vmem((SUB, 128), BF),
            vmem((16, SUB, 128), BF),
            vmem((BLK, 128), F32),
            vmem((16, 256), F32),
            vmem((16, 16, 256), BF),
            vmem((16, 1, 256), F32),
            vmem((32, 1, 256), F32),
            vmem((TOK, D), F32),
            vmem((TOK, 1), F32),
            sem((6,)),
            sem((5, 2, 4)),
            sem((5, 4)),
            sem((5, 4)),
            sem((5, 5)),
            sem((5,)),
            sem((5,)),
            sem((3,)),
            sem((3,)),
            sem((2, 6)),
            sem((2, 6)),
            sem((2,)),
            sem((2,)),
        ],
        compiler_params=pltpu.CompilerParams(
            collective_id=0, has_side_effects=True, vmem_limit_bytes=56 * 1024 * 1024
        ),
        name="block_pair",
    )(
        tokens.reshape(TOK, D), norm_gains, qkv_space.T, out_space.T, qkv_time.T, out_time.T,
        cotangent.reshape(16, 8, D),
    )
    return (
        result.reshape(1, 16, 8, D),
        d_tokens.reshape(1, 1, TOK, D),
        d_space.T,
        d_time.T,
        d_gain,
    )


def solution(mesh):
    return jax.shard_map(
        local,
        mesh=mesh,
        in_specs=(
            P("dp", "seq", None, None),
            P(),
            P(None, "seq"),
            P(None, "seq"),
            P(None, "seq"),
            P(None, "seq"),
            P("dp", None, "seq", None),
        ),
        out_specs=(
            P("dp", None, "seq", None),
            P("dp", "seq", None, None),
            P(None, "seq"),
            P(None, "seq"),
            P(None, "seq"),
        ),
        check_vma=False,
    )
```
